256 devices in a mesh: sector: 128 (over x_hi, y, z, core), span: 2 (over x_lo).
Axes of the slice: x: 4 (x_hi: 2, x_lo: 2; x = x_hi * 2 + x_lo), y: 4, z: 8, core: 2. Of those that a mesh axis runs over, the one named last changes fastest.
Arguments:
- flow: float32 [2, 6, 8, 16, 65536], P(None, None, None, 'span', 'sector'), may hold values from -0.8 to 3.8, as said below
- offsets: int32 [2], replicated, may hold values from 0 to 511
- intersections: int32 [2, 4, 2], replicated, may hold values from 0 to 4
- weights: float32 [2, 4, 2, 128, 128], replicated, may hold values from 0.001 to 1
Outputs:
- advanced: float32 [2, 5, 8, 16, 65536], P(None, None, None, 'span', 'sector')
The draws below stay inside these ranges and needn't reach their ends.
Inputs may be any that keep to these rules, and one draw needn't show every extreme that they name: Each entry of offsets is a rotation of the rotor cycle in face blocks, less than 512. Each entry of intersections names one of the 5 blocks of a stator sector's intersection slice. `flow`: density lies between 0.7 and 1.3, each momentum component within 0.8 in magnitude, total energy between 2.4 and 3.8, eddy viscosity between 0.005 and 0.3.
All inputs are finite; a program needn't handle non-finite values.
Results may differ from the reference program's by a relative error of at most 0.00005.
Values sent between devices are 32-bit elements; how exact they have to be, the bound alone decides.
No kernel may reach another device: no remote copies, remote signals or barrier semaphores. Data moves between devices by JAX's collectives and lax.ppermute only.
A program may use at most 64 MiB of HBM per device.

```python
import math
import jax
import jax.numpy as jnp
from jax import lax

W = 128
FB = 4
AX = 8
R = 16
NT = 65536
N_SECTOR = 128


def draw_flow(key, part):
    key = jax.random.fold_in(key, 11)
    subkeys = jax.random.split(key, 4)
    grid_shape = (2, AX, R, NT)
    momentum_shape = (2, 3, AX, R, NT)
    density = jax.random.uniform(subkeys[0], grid_shape, jnp.float32, 0.8, 1.2)
    momentum = jnp.clip(0.3 * jax.random.normal(subkeys[1], momentum_shape, jnp.float32), -0.8, 0.8)
    energy = jax.random.uniform(subkeys[2], grid_shape, jnp.float32, 2.5, 3.5)
    eddy = jnp.exp(jax.random.uniform(subkeys[3], grid_shape, jnp.float32, math.log(0.01), math.log(0.2)))
    return jnp.concatenate([density[:, None], momentum, energy[:, None], eddy[:, None]], axis=1)


def set_ends(result, rng, smallest, high):
    shape = result.shape
    place = [jax.random.randint(jax.random.fold_in(rng, axis), (), 0, shape[axis]) for axis in range(len(shape))]
    result = result.at[tuple(place)].set(smallest)
    longest = shape.index(max(shape))
    place[longest] = (place[longest] + 1) % shape[longest]
    return result.at[tuple(place)].set(high)


def setup_inputs(seed: int = 0) -> dict:
    keys = jax.random.split(jax.random.key(seed), 5)
    flow = draw_flow(jax.random.fold_in(keys[4], 71), 0)
    offsets = jax.random.randint(keys[1], (2,), 0, N_SECTOR * FB).astype(jnp.int32)
    intersections = set_ends(jax.random.randint(keys[2], (2, FB, 2), 0, FB + 1), jax.random.fold_in(keys[2], 1), 0, FB).astype(jnp.int32)
    weights = jnp.clip(jnp.exp(jax.random.uniform(keys[3], (2, FB, 2, W, W), jnp.float32, math.log(0.001), math.log(1.0))), 0.001, 1.0)
    return dict(flow=flow, offsets=offsets, intersections=intersections, weights=weights)


GAMMA = 1.4
sigma_base = 0.05
step_size = 0.25
blend_weight = 1.0
highest = lax.Precision.HIGHEST


def physical_flux(fields, direction):
    density = fields[:, 0]
    inverse = 1.0 / density
    normal_momentum = fields[:, 1 + direction]
    velocity = normal_momentum * inverse
    kinetic = 0.5 * (fields[:, 1] * fields[:, 1] + fields[:, 2] * fields[:, 2] + fields[:, 3] * fields[:, 3]) * inverse
    pressure = (GAMMA - 1.0) * (fields[:, 4] - kinetic)
    pieces = [normal_momentum]
    for component in range(3):
        summand = fields[:, 1 + component] * velocity
        if component == direction:
            summand = summand + pressure
        pieces.append(summand)
    pieces.append((fields[:, 4] + pressure) * velocity)
    return jnp.stack(pieces, axis=1)


def face_flux(lower_side, upper_side, lower_eddy, upper_eddy, direction):
    average = 0.5 * (lower_side + upper_side)
    damping = sigma_base + 0.5 * (lower_eddy + upper_eddy)
    return physical_flux(average, direction) - jnp.expand_dims(damping, 1) * (upper_side - lower_side)


def flux_difference(padded, eddy_padded, direction, axis_number, retained=None):
    face_count = padded.shape[axis_number] - 1
    lower_side = lax.slice_in_dim(padded, 0, face_count, axis=axis_number)
    upper_side = lax.slice_in_dim(padded, 1, face_count + 1, axis=axis_number)
    lower_eddy = lax.slice_in_dim(eddy_padded, 0, face_count, axis=axis_number - 1)
    upper_eddy = lax.slice_in_dim(eddy_padded, 1, face_count + 1, axis=axis_number - 1)
    fluxes = face_flux(lower_side, upper_side, lower_eddy, upper_eddy, direction)
    if retained is not None:
        fluxes = fluxes * retained
    return lax.slice_in_dim(fluxes, 1, face_count, axis=axis_number) - lax.slice_in_dim(fluxes, 0, face_count - 1, axis=axis_number)


def axial_part(fields, eddy, ghost_in, ghost_out):
    rotor_column = jnp.concatenate([fields[0:1, :, :1], fields[0:1], ghost_out[None, :, None]], axis=2)
    stator_column = jnp.concatenate([ghost_in[None, :, None], fields[1:2], fields[1:2, :, -1:]], axis=2)
    padded = jnp.concatenate([rotor_column, stator_column], axis=0)
    eddy_padded = jnp.concatenate([eddy[:, :1], eddy, eddy[:, -1:]], axis=1)
    return flux_difference(padded, eddy_padded, 2, 2)


def interface_ghosts(fields, offset, intersection_list, weight_table):
    blocks = weight_table.shape[0]
    width = weight_table.shape[2]
    radial = fields.shape[3]
    sectors = fields.shape[4] // (blocks * width)
    rotor_face = fields[0, :, -1].reshape(5, radial, sectors, blocks, width)
    stator_face = fields[1, :, 0].reshape(5, radial, sectors, blocks, width)
    turn_count = offset // blocks
    within = offset % blocks
    start = (blocks - within - 1).astype(jnp.int32)
    shifted = jnp.roll(rotor_face, turn_count, axis=2)
    prior = jnp.roll(shifted, 1, axis=2)
    window = jnp.concatenate([prior, shifted], axis=3)
    sliced = lax.dynamic_slice_in_dim(window, start, blocks + 1, axis=3)
    selector = (intersection_list[:, :, None] == jnp.arange(blocks + 1, dtype=jnp.int32)[None, None, :]).astype(jnp.float32)
    chosen = jnp.einsum('crnix,jmi->crnjmx', sliced, selector, precision=highest)
    numer = jnp.einsum('crnjmx,jmex->crnje', chosen, weight_table, precision=highest)
    denom = jnp.sum(weight_table, axis=(1, 3))
    ghost_in = (numer / denom).reshape(5, radial, sectors * blocks * width)
    contrib = jnp.einsum('crnje,jmex->crnjmx', stator_face, weight_table, precision=highest)
    back = jnp.einsum('crnjmx,jmi->crnix', contrib, selector, precision=highest)
    dsum = jnp.einsum('jmex,jmi->ix', weight_table, selector, precision=highest)
    back_window = lax.dynamic_update_slice_in_dim(jnp.zeros(window.shape, back.dtype), back, start, axis=3)
    dsum_window = lax.dynamic_update_slice_in_dim(jnp.zeros((2 * blocks, width), dsum.dtype), dsum, start, axis=0)
    combined = back_window[:, :, :, blocks:] + jnp.roll(back_window[:, :, :, :blocks], -1, axis=2)
    returned = jnp.roll(combined, -turn_count, axis=2)
    den_rotor = dsum_window[blocks:] + dsum_window[:blocks]
    ghost_out = ((returned + blend_weight * rotor_face) / (den_rotor + blend_weight)).reshape(5, radial, sectors * blocks * width)
    return ghost_in, ghost_out


def residual(fields, eddy, ghost_in, ghost_out, retained):
    beside_all = jnp.concatenate([fields[..., -1:], fields, fields[..., :1]], axis=4)
    eddy_around = jnp.concatenate([eddy[..., -1:], eddy, eddy[..., :1]], axis=3)
    total = flux_difference(beside_all, eddy_around, 0, 4)
    zero_plane = jnp.zeros_like(fields[:, :, :, :1])
    across = jnp.concatenate([zero_plane, fields, zero_plane], axis=3)
    eddy_zero = jnp.zeros_like(eddy[:, :, :1])
    eddy_across = jnp.concatenate([eddy_zero, eddy, eddy_zero], axis=2)
    total = total + flux_difference(across, eddy_across, 1, 3, retained)
    total = total + axial_part(fields, eddy, ghost_in, ghost_out)
    return -total


def reference(flow, offsets, intersections, weights):
    state = flow[:, :5]
    eddy = flow[:, 5]
    radial = flow.shape[3]
    face_index = jnp.arange(radial + 1, dtype=jnp.int32)
    retained = ((face_index > 0) & (face_index < radial)).astype(flow.dtype)[:, None]
    ghost_in, ghost_out = interface_ghosts(state, offsets[0], intersections[0], weights[0])
    middle = state + 0.5 * step_size * residual(state, eddy, ghost_in, ghost_out, retained)
    ghost_in, ghost_out = interface_ghosts(middle, offsets[1], intersections[1], weights[1])
    return state + step_size * residual(middle, eddy, ghost_in, ghost_out, retained)
```

```python
import functools

import jax
import jax.numpy as jnp
from jax import lax
from jax.experimental import pallas as pl
from jax.experimental.pallas import tpu as pltpu
from jax.sharding import PartitionSpec as P

HIGHEST = lax.Precision.HIGHEST
VMEM_LIMIT = 40 * 1024 * 1024
NP, NR, NB, W = 8, 8, 4, 128
NC = NB * W


def face(a, b, damping, d):
    s = [x + y for x, y in zip(a, b)]
    inv = 1.0 / s[0]
    u = s[1 + d] * inv
    p = 0.4 * (s[4] - 0.5 * (s[1] * s[1] + s[2] * s[2] + s[3] * s[3]) * inv)
    f = [s[1 + d]] + [s[1 + c] * u + p if c == d else s[1 + c] * u for c in range(3)]
    f.append((s[4] + p) * u)
    return [g - damping * (y - x) for g, x, y in zip(f, a, b)]


def pack_edges(q_ref, nf, h, re_ref, le_ref, rad_ref):
    lane = lax.broadcasted_iota(jnp.int32, (NR, W), 1)

    def plane(p, tiles):
        re, le = tiles
        row, a = p // NP, p % NP
        for f in range(nf):
            at = f * 16 + p
            hit = lane == at
            re = jnp.where(hit, pltpu.roll(q_ref[row, f, a, :, NC - W : NC], lax.rem(at + 1, W), 1), re)
            le = jnp.where(hit, pltpu.roll(q_ref[row, f, a, :, 0:W], at, 1), le)
            rad_ref[row * nf + f, pl.ds(a, 1), :] = q_ref[row, f, a, pl.ds(h, 1), :]
        return re, le

    zero = jnp.zeros((NR, W), jnp.float32)
    re_ref[...], le_ref[...] = lax.fori_loop(0, 2 * NP, plane, (zero, zero))


def pack_faces(q_ref, pm_ref, sm_ref):
    for b in range(NB):
        for c in range(5):
            pm_ref[b, c] = q_ref[0, c, NP - 1, :, b * W : (b + 1) * W]
            sm_ref[b, c] = q_ref[1, c, 0, :, b * W : (b + 1) * W]


def pack_kernel(span_ref, q_ref, pm_ref, sm_ref, em_ref, re_ref, le_ref, rad_ref):
    pack_faces(q_ref, pm_ref, sm_ref)
    for b in range(NB):
        em_ref[0, b] = q_ref[0, 5, NP - 1, :, b * W : (b + 1) * W]
        em_ref[1, b] = q_ref[1, 5, 0, :, b * W : (b + 1) * W]
    pack_edges(q_ref, 6, jnp.where(span_ref[0] == 0, NR - 1, 0), re_ref, le_ref, rad_ref)


def bulk_kernel(scale, nf, span_ref, flow_ref, q_ref, re_ref, lh_ref, rh_ref, rad_ref, re0_ref, lh0_ref, rh0_ref, rad0_ref, out_ref):
    span = span_ref[0]
    lower = span == 0
    sgn = jnp.where(lower, 1.0, -1.0)
    halo_row = jnp.where(lower, NR - 1, 0)
    toward = jnp.where(lower, NR - 1, 1)
    back = jnp.where(lower, 1, NR - 1)
    lane = lax.broadcasted_iota(jnp.int32, (NR, W), 1)
    sub = lax.broadcasted_iota(jnp.int32, (NR, NC), 0)
    at_halo = sub == halo_row
    at_wall = sub == NR - 1 - halo_row

    def lanes(tile, f):
        return tile if f == 0 else pltpu.roll(tile, W - 16 * f, 1)

    own, beyond = re_ref[...], rh_ref[...]
    last = face(
        [lanes(own, f) for f in range(5)],
        [lanes(beyond, f) for f in range(5)],
        0.1 + lanes(re0_ref[...], 5) + lanes(rh0_ref[...], 5),
        0,
    )
    left, left0 = lh_ref[...], lh0_ref[...]

    def left_of(x, tile, at):
        t = pltpu.roll(tile, lax.rem(W - at, W), 1)
        y = pltpu.roll(x, 1, 1)
        return jnp.concatenate([jnp.where(lane == 0, t, y[:, :W]), y[:, W:]], axis=1)

    def beside(x, halo):
        return jnp.where(at_halo, halo, pltpu.roll(x, toward, 0))

    for row in range(2):

        def plane(a, below, row=row):
            p = row * NP + a
            x = [q_ref[row, f, a] for f in range(5)]
            e = flow_ref[row, 5, a]
            up = jnp.minimum(a + 1, NP - 1)
            above = face(x, [q_ref[row, f, up] for f in range(5)], 0.1 + e + flow_ref[row, 5, up], 2)
            if row == 0:
                keep = jnp.where(a == NP - 1, 0.0, 1.0)
                above = [g * keep for g in above]
            total = [g - l for g, l in zip(above, below)]
            near = [beside(x[f], rad_ref[row * nf + f, pl.ds(a, 1), :]) for f in range(5)]
            e_near = beside(e, rad0_ref[row * 6 + 5, pl.ds(a, 1), :])
            s_damp = sgn * (0.1 + e + e_near)
            g = face(x, near, s_damp, 1)
            for f in range(5):
                other = jnp.where(at_wall, 0.0, pltpu.roll(g[f], back, 0))
                total[f] = total[f] + sgn * (g[f] - other)
            lo = [left_of(x[f], left, f * 16 + p) for f in range(5)]
            e_lo = left_of(e, left0, 80 + p)
            g = face(lo, x, 0.1 + e + e_lo, 0)
            for f in range(5):
                y = pltpu.roll(g[f], NC - 1, 1)
                t = pltpu.roll(last[f], W - 1 - p, 1)
                y = jnp.concatenate([y[:, : NC - W], jnp.where(lane == W - 1, t, y[:, NC - W :])], axis=1)
                total[f] = total[f] + (y - g[f])
            for f in range(5):
                out_ref[row, f, a] = flow_ref[row, f, a] - (0.5 * scale) * total[f]
            return above

        if row == 0:
            x0 = [q_ref[0, f, 0] for f in range(5)]
            first = face(x0, x0, jnp.zeros((NR, NC), jnp.float32), 2)
        else:
            first = [jnp.zeros((NR, NC), jnp.float32)] * 5
        lax.fori_loop(0, NP, plane, first)


def ghost_kernel(scale, last, sc_ref, span_ref, idx_ref, part_ref, pm_ref, sm_ref, em_ref, px_ref, py_ref, pz_ref,
                 sx_ref, sy_ref, sz_ref, w_ref, *rest):
    if last:
        out_ref, win, acc = rest
    else:
        out_ref, pm_out, sm_out, re_out, le_out, rad_out, win, acc = rest
    f0 = sc_ref[0] % NB
    odd = (sc_ref[0] // NB) % 2 == 1
    start = NB - 1 - f0
    win[NB : 2 * NB] = jnp.where(odd, py_ref[...], px_ref[...])
    win[0:NB] = jnp.where(odd, pz_ref[...], py_ref[...])
    acc[...] = jnp.zeros(acc.shape, jnp.float32)
    ones = jnp.ones((8, W), jnp.float32)
    out_ref[...] = part_ref[...]
    for j in range(NB):
        wj = jnp.concatenate([w_ref[j, 0], w_ref[j, 1]], axis=1)
        lhs = jnp.concatenate(
            [
                jnp.concatenate([win[start + idx_ref[j, m]].reshape(40, W), ones], axis=0)
                for m in range(2)
            ],
            axis=1,
        )
        num = lax.dot_general(lhs, wj, (((1,), (1,)), ((), ())), precision=HIGHEST, preferred_element_type=jnp.float32)
        inv = 1.0 / num[40:48]
        ghost = [num[8 * c : 8 * c + 8] * inv for c in range(5)]
        g = face(ghost, [sm_ref[j, c] for c in range(5)], 0.1 + 2.0 * em_ref[1, j], 2)
        for c in range(5):
            cells = (1, c, 0, slice(None), slice(j * W, (j + 1) * W))
            out_ref[cells] = part_ref[cells] + (0.5 * scale) * g[c]
        s1 = jnp.where(odd, sy_ref[j], sx_ref[j]).reshape(40, W)
        s2 = jnp.where(odd, sz_ref[j], sy_ref[j]).reshape(40, W)
        r = lax.dot_general(
            jnp.concatenate([s1, s2, ones], axis=0), wj, (((1,), (0,)), ((), ())),
            precision=HIGHEST, preferred_element_type=jnp.float32,
        )
        for m in range(2):
            rm = r[:, m * W : (m + 1) * W]
            b1 = idx_ref[j, m] + 3 - f0
            acc[b1, 0:40] += rm[0:40]
            acc[b1, 40:48] += rm[80:88]
            acc[b1 + 4, 0:40] += rm[40:80]
            acc[b1 + 4, 40:48] += rm[80:88]
    for b in range(NB):
        inv = 1.0 / (acc[4 + b, 40:48] + 1.0)
        own = [pm_ref[b, c] for c in range(5)]
        ghost = [(acc[4 + b, 8 * c : 8 * c + 8] + own[c]) * inv for c in range(5)]
        g = face(own, ghost, 0.1 + 2.0 * em_ref[0, b], 2)
        for c in range(5):
            cells = (0, c, NP - 1, slice(None), slice(b * W, (b + 1) * W))
            out_ref[cells] = part_ref[cells] - (0.5 * scale) * g[c]
    if not last:
        pack_faces(out_ref, pm_out, sm_out)
        pack_edges(out_ref, 5, jnp.where(span_ref[0] == 0, NR - 1, 0), re_out, le_out, rad_out)


SMEM = pl.BlockSpec(memory_space=pltpu.SMEM)
VMEM = pl.BlockSpec(memory_space=pltpu.VMEM)
PARAMS = pltpu.CompilerParams(vmem_limit_bytes=VMEM_LIMIT)


def arr(*shape):
    return jax.ShapeDtypeStruct(shape, jnp.float32)


FACE = (NB, 5, NR, W)
TILE = (NR, W)
STATE = (2, 5, NP, NR, NC)


def perm(x, d):
    n = lax.axis_size("sector")
    return lax.ppermute(x, "sector", [(i, (i + d) % n) for i in range(n)])


def both(d):
    if d == 0:
        return lambda p, s: (p, s)
    return lambda p, s: (perm(p, d), perm(s, -d))


def exchange(pm, sm, offset):
    k = offset // NB
    p, s = lax.switch((k >> 1) & 7, [both(2 * i) for i in range(8)], pm, sm)
    p, s = lax.switch((k >> 4) & 7, [both(16 * i) for i in range(8)], p, s)
    py, sy = perm(p, 1), perm(s, -1)
    pz, sz = lax.cond(k & 1 == 1, both(2), both(0), p, s)
    return (p, py, pz), (s, sy, sz)


def halos(re, le, rad):
    return perm(re, 1), perm(le, -1), lax.ppermute(rad, "span", [(0, 1), (1, 0)])


def local(flow, offsets, intersections, weights):
    span = lax.axis_index("span").astype(jnp.int32).reshape(1)
    pm, sm, em, re, le, rad = pl.pallas_call(
        pack_kernel,
        in_specs=[SMEM, VMEM],
        out_specs=[VMEM] * 6,
        out_shape=[arr(*FACE), arr(*FACE), arr(2, NB, NR, W), arr(*TILE), arr(*TILE), arr(12, NP, NC)],
        compiler_params=PARAMS,
        name="pack",
    )(span, flow)
    q, nf = flow, 6
    first = None
    for step, scale in enumerate((0.125, 0.25)):
        lh, rh, radh = halos(re, le, rad)
        if first is None:
            first = (re, lh, rh, radh)
        ps, ss = exchange(pm, sm, offsets[step])
        part = pl.pallas_call(
            functools.partial(bulk_kernel, scale, nf),
            in_specs=[SMEM] + [VMEM] * 10,
            out_specs=VMEM,
            out_shape=arr(*STATE),
            compiler_params=PARAMS,
            cost_estimate=pl.CostEstimate(flops=20_000_000, bytes_accessed=8_000_000, transcendentals=0),
            name="bulk",
        )(span, flow, q, re, lh, rh, radh, *first)
        last = step == 1
        outs = [arr(*STATE)]
        if not last:
            outs += [arr(*FACE), arr(*FACE), arr(*TILE), arr(*TILE), arr(10, NP, NC)]
        res = pl.pallas_call(
            functools.partial(ghost_kernel, scale, last),
            in_specs=[SMEM] * 3 + [VMEM] * 11,
            out_specs=[VMEM] * len(outs),
            out_shape=outs,
            scratch_shapes=[pltpu.VMEM((2 * NB, 5, NR, W), jnp.float32), pltpu.VMEM((3 * NB, 48, W), jnp.float32)],
            compiler_params=PARAMS,
            name="ghost",
        )(offsets[step].reshape(1), span, intersections[step], part, pm, sm, em, *ps, *ss, weights[step])
        if last:
            return res[0]
        q, pm, sm, re, le, rad = res
        nf = 5


def solution(mesh):
    return jax.shard_map(
        local,
        mesh=mesh,
        in_specs=(P(None, None, None, "span", "sector"), P(), P(), P()),
        out_specs=P(None, None, None, "span", "sector"),
        check_vma=False,
    )
```

```python
import functools

import jax
import jax.numpy as jnp
from jax import lax
from jax.experimental import pallas as pl
from jax.experimental.pallas import tpu as pltpu
from jax.sharding import PartitionSpec as P

HIGHEST = lax.Precision.HIGHEST
VMEM_LIMIT = 40 * 1024 * 1024
NP, NR, NB, W = 8, 8, 4, 128
NC = NB * W


def face(a, b, damping, d):
    s = [x + y for x, y in zip(a, b)]
    inv = 1.0 / s[0]
    u = s[1 + d] * inv
    p = 0.4 * (s[4] - 0.5 * (s[1] * s[1] + s[2] * s[2] + s[3] * s[3]) * inv)
    f = [s[1 + d]] + [s[1 + c] * u + p if c == d else s[1 + c] * u for c in range(3)]
    f.append((s[4] + p) * u)
    return [g - damping * (y - x) for g, x, y in zip(f, a, b)]


def pack_edges(q_ref, nf, h, re_ref, le_ref, rad_ref):
    lane = lax.broadcasted_iota(jnp.int32, (NR, W), 1)

    def plane(p, tiles):
        re, le = tiles
        row, a = p // NP, p % NP
        for f in range(nf):
            at = f * 16 + p
            hit = lane == at
            re = jnp.where(hit, pltpu.roll(q_ref[row, f, a, :, NC - W : NC], lax.rem(at + 1, W), 1), re)
            le = jnp.where(hit, pltpu.roll(q_ref[row, f, a, :, 0:W], at, 1), le)
            rad_ref[row * nf + f, pl.ds(a, 1), :] = q_ref[row, f, a, pl.ds(h, 1), :]
        return re, le

    zero = jnp.zeros((NR, W), jnp.float32)
    re_ref[...], le_ref[...] = lax.fori_loop(0, 2 * NP, plane, (zero, zero))


def pack_faces(q_ref, pm_ref, sm_ref):
    for b in range(NB):
        for c in range(5):
            pm_ref[b * 5 + c] = q_ref[0, c, NP - 1, :, b * W : (b + 1) * W]
            sm_ref[b * 5 + c] = q_ref[1, c, 0, :, b * W : (b + 1) * W]


def faces_kernel(flow_ref, pm_ref, sm_ref, em_ref, buf, sem):
    cps = [
        pltpu.make_async_copy(flow_ref.at[0, :, NP - 1], buf.at[0], sem.at[0]),
        pltpu.make_async_copy(flow_ref.at[1, :, 0], buf.at[1], sem.at[1]),
    ]
    for cp in cps:
        cp.start()
    for cp in cps:
        cp.wait()
    for b in range(NB):
        cells = slice(b * W, (b + 1) * W)
        for c in range(5):
            pm_ref[b * 5 + c] = buf[0, c, :, cells]
            sm_ref[b * 5 + c] = buf[1, c, :, cells]
        em_ref[0, b] = buf[0, 5, :, cells]
        em_ref[1, b] = buf[1, 5, :, cells]


def edges_kernel(span_ref, q_ref, re_ref, le_ref, rad_ref):
    pack_edges(q_ref, 6, jnp.where(span_ref[0] == 0, NR - 1, 0), re_ref, le_ref, rad_ref)


def bulk_kernel(scale, flow_ref, q_ref, out_ref):
    lane = lax.broadcasted_iota(jnp.int32, (NR, W), 1)
    sub = lax.broadcasted_iota(jnp.int32, (NR, NC), 0)

    def no_first(g):
        return jnp.concatenate([jnp.where(lane == 0, 0.0, g[:, :W]), g[:, W:]], axis=1)

    for row in range(2):

        def plane(a, below, row=row):
            x = [q_ref[row, f, a] for f in range(5)]
            e = flow_ref[row, 5, a]
            up = jnp.minimum(a + 1, NP - 1)
            above = face(x, [q_ref[row, f, up] for f in range(5)], 0.1 + e + flow_ref[row, 5, up], 2)
            if row == 0:
                keep = jnp.where(a == NP - 1, 0.0, 1.0)
                above = [g * keep for g in above]
            total = [g - l for g, l in zip(above, below)]
            lo = [pltpu.roll(v, 1, 0) for v in x]
            g = face(lo, x, 0.1 + e + pltpu.roll(e, 1, 0), 1)
            g = [jnp.where(sub == 0, 0.0, v) for v in g]
            total = [t + (pltpu.roll(v, NR - 1, 0) - v) for t, v in zip(total, g)]
            lo = [pltpu.roll(v, 1, 1) for v in x]
            g = face(lo, x, 0.1 + e + pltpu.roll(e, 1, 1), 0)
            g = [no_first(v) for v in g]
            total = [t + (pltpu.roll(v, NC - 1, 1) - v) for t, v in zip(total, g)]
            for f in range(5):
                out_ref[row, f, a] = flow_ref[row, f, a] - (0.5 * scale) * total[f]
            return above

        if row == 0:
            x0 = [q_ref[0, f, 0] for f in range(5)]
            first = face(x0, x0, jnp.zeros((NR, NC), jnp.float32), 2)
        else:
            first = [jnp.zeros((NR, NC), jnp.float32)] * 5
        lax.fori_loop(0, NP, plane, first)


def finish_kernel(scale, last, nf, sc_ref, span_ref, idx_ref, part_ref, pm_ref, sm_ref, em_ref, px_ref, sx_ref, up_ref, down_ref,
                  re_ref, le_ref, rad_ref, radh_ref, up0_ref, down0_ref, re0_ref, le0_ref, rad0_ref, radh0_ref, w_ref, *rest):
    if last:
        out_ref, win, acc, rfix = rest
    else:
        out_ref, pm_out, sm_out, re_out, le_out, rad_out, win, acc, rfix = rest
    half = 0.5 * scale
    f0 = sc_ref[0] % NB
    odd = (sc_ref[0] // NB) % 2 == 1
    start = NB - 1 - f0
    nface = 5 * NB
    lower = span_ref[0] == 0
    sgn = jnp.where(lower, 1.0, -1.0)
    h = jnp.where(lower, NR - 1, 0)

    for row in range(2):
        own = [rad_ref[row * nf + f] for f in range(5)]
        other = [radh_ref[row * nf + f] for f in range(5)]
        damp = sgn * (0.1 + rad0_ref[row * 6 + 5] + radh0_ref[row * 6 + 5])
        g = face(own, other, damp, 1)
        for f in range(5):
            rfix[row * 5 + f] = (-half * sgn) * g[f]

    def lanes(tile, f):
        return tile if f == 0 else pltpu.roll(tile, W - 16 * f, 1)

    def both_sides(lo, hi, lo0, hi0):
        g = face([lanes(lo, f) for f in range(5)], [lanes(hi, f) for f in range(5)], 0.1 + lanes(lo0, 5) + lanes(hi0, 5), 0)
        return [half * v for v in g]

    left = both_sides(up_ref[nface], le_ref[...], up0_ref[nface], le0_ref[...])
    right = both_sides(re_ref[...], down_ref[nface], re0_ref[...], down0_ref[nface])
    lane = lax.broadcasted_iota(jnp.int32, (NR, W), 1)
    at_h = lax.broadcasted_iota(jnp.int32, (NR, NC), 0) == h

    def plane(p, carry):
        row, a = p // NP, p % NP
        for f in range(5):
            v = part_ref[row, f, a] + jnp.where(at_h, rfix[row * 5 + f, pl.ds(a, 1), :], 0.0)
            lo = jnp.where(lane == 0, pltpu.roll(left[f], lax.rem(W - p, W), 1), 0.0)
            hi = jnp.where(lane == W - 1, pltpu.roll(right[f], W - 1 - p, 1), 0.0)
            out_ref[row, f, a] = jnp.concatenate([v[:, :W] + lo, v[:, W : NC - W], v[:, NC - W :] - hi], axis=1)
        return carry

    lax.fori_loop(0, 2 * NP, plane, 0)

    win[NB : 2 * NB] = jnp.where(odd, down_ref[0:nface], px_ref[...]).reshape(NB, 5, NR, W)
    win[0:NB] = jnp.where(odd, px_ref[...], up_ref[0:nface]).reshape(NB, 5, NR, W)
    acc[...] = jnp.zeros(acc.shape, jnp.float32)
    ones = jnp.ones((8, W), jnp.float32)
    for j in range(NB):
        wj = jnp.concatenate([w_ref[j, 0], w_ref[j, 1]], axis=1)
        lhs = jnp.concatenate(
            [
                jnp.concatenate([win[start + idx_ref[j, m]].reshape(40, W), ones], axis=0)
                for m in range(2)
            ],
            axis=1,
        )
        num = lax.dot_general(lhs, wj, (((1,), (1,)), ((), ())), precision=HIGHEST, preferred_element_type=jnp.float32)
        inv = 1.0 / num[40:48]
        ghost = [num[8 * c : 8 * c + 8] * inv for c in range(5)]
        g = face(ghost, [sm_ref[j * 5 + c] for c in range(5)], 0.1 + 2.0 * em_ref[1, j], 2)
        for c in range(5):
            cells = (1, c, 0, slice(None), slice(j * W, (j + 1) * W))
            out_ref[cells] = out_ref[cells] + half * g[c]
        blk = slice(j * 5, j * 5 + 5)
        s1 = jnp.where(odd, up_ref[blk], sx_ref[blk]).reshape(40, W)
        s2 = jnp.where(odd, sx_ref[blk], down_ref[blk]).reshape(40, W)
        r = lax.dot_general(
            jnp.concatenate([s1, s2, ones], axis=0), wj, (((1,), (0,)), ((), ())),
            precision=HIGHEST, preferred_element_type=jnp.float32,
        )
        for m in range(2):
            rm = r[:, m * W : (m + 1) * W]
            b1 = idx_ref[j, m] + 3 - f0
            acc[b1, 0:40] += rm[0:40]
            acc[b1, 40:48] += rm[80:88]
            acc[b1 + 4, 0:40] += rm[40:80]
            acc[b1 + 4, 40:48] += rm[80:88]
    for b in range(NB):
        inv = 1.0 / (acc[4 + b, 40:48] + 1.0)
        own = [pm_ref[b * 5 + c] for c in range(5)]
        ghost = [(acc[4 + b, 8 * c : 8 * c + 8] + own[c]) * inv for c in range(5)]
        g = face(own, ghost, 0.1 + 2.0 * em_ref[0, b], 2)
        for c in range(5):
            cells = (0, c, NP - 1, slice(None), slice(b * W, (b + 1) * W))
            out_ref[cells] = out_ref[cells] - half * g[c]
    if not last:
        pack_faces(out_ref, pm_out, sm_out)
        pack_edges(out_ref, 5, h, re_out, le_out, rad_out)


SMEM = pl.BlockSpec(memory_space=pltpu.SMEM)
VMEM = pl.BlockSpec(memory_space=pltpu.VMEM)
PARAMS = pltpu.CompilerParams(vmem_limit_bytes=VMEM_LIMIT)


def arr(*shape):
    return jax.ShapeDtypeStruct(shape, jnp.float32)


FACE = (NB * 5, NR, W)
TILE = (NR, W)
STATE = (2, 5, NP, NR, NC)


def perm(x, d):
    n = lax.axis_size("sector")
    return lax.ppermute(x, "sector", [(i, (i + d) % n) for i in range(n)])


def both(d):
    if d == 0:
        return lambda p, s: (p, s)
    return lambda p, s: (perm(p, d), perm(s, -d))


def exchange(pm, sm, re, le, offset):
    k = offset // NB
    odd = (k & 1) == 1
    half = (k + 1) >> 1
    p, s = lax.switch(half & 7, [both(2 * i) for i in range(8)], pm, sm)
    p, s = lax.switch((half >> 3) & 7, [both(16 * i) for i in range(8)], p, s)
    up = perm(jnp.concatenate([jnp.where(odd, s, p), re[None]]), 1)
    down = perm(jnp.concatenate([jnp.where(odd, p, s), le[None]]), -1)
    return p, s, up, down


def local(flow, offsets, intersections, weights):
    span = lax.axis_index("span").astype(jnp.int32).reshape(1)
    pm, sm, em = pl.pallas_call(
        faces_kernel,
        in_specs=[pl.BlockSpec(memory_space=pl.ANY)],
        out_specs=[VMEM] * 3,
        out_shape=[arr(*FACE), arr(*FACE), arr(2, NB, NR, W)],
        scratch_shapes=[pltpu.VMEM((2, 6, NR, NC), jnp.float32), pltpu.SemaphoreType.DMA((2,))],
        compiler_params=PARAMS,
        name="faces",
    )(flow)
    re, le, rad = pl.pallas_call(
        edges_kernel,
        in_specs=[SMEM, VMEM],
        out_specs=[VMEM] * 3,
        out_shape=[arr(*TILE), arr(*TILE), arr(12, NP, NC)],
        compiler_params=PARAMS,
        name="edges",
    )(span, flow)
    q, nf = flow, 6
    first = None
    for step, scale in enumerate((0.125, 0.25)):
        radh = lax.ppermute(rad, "span", [(0, 1), (1, 0)])
        px, sx, up, down = exchange(pm, sm, re, le, offsets[step])
        part = pl.pallas_call(
            functools.partial(bulk_kernel, scale),
            in_specs=[VMEM] * 2,
            out_specs=VMEM,
            out_shape=arr(*STATE),
            compiler_params=PARAMS,
            cost_estimate=pl.CostEstimate(flops=20_000_000, bytes_accessed=8_000_000, transcendentals=0),
            name="bulk",
        )(flow, q)
        edges = (re, le, rad, radh)
        if first is None:
            first = (up, down) + edges
        last = step == 1
        outs = [arr(*STATE)]
        if not last:
            outs += [arr(*FACE), arr(*FACE), arr(*TILE), arr(*TILE), arr(10, NP, NC)]
        res = pl.pallas_call(
            functools.partial(finish_kernel, scale, last, nf),
            in_specs=[SMEM] * 3 + [VMEM] * 19,
            out_specs=[VMEM] * len(outs),
            out_shape=outs,
            scratch_shapes=[
                pltpu.VMEM((2 * NB, 5, NR, W), jnp.float32),
                pltpu.VMEM((3 * NB, 48, W), jnp.float32),
                pltpu.VMEM((10, NP, NC), jnp.float32),
            ],
            compiler_params=PARAMS,
            name="finish",
        )(offsets[step].reshape(1), span, intersections[step], part, pm, sm, em, px, sx, up, down, *edges, *first, weights[step])
        if last:
            return res[0]
        q, pm, sm, re, le, rad = res
        nf = 5


def solution(mesh):
    return jax.shard_map(
        local,
        mesh=mesh,
        in_specs=(P(None, None, None, "span", "sector"), P(), P(), P()),
        out_specs=P(None, None, None, "span", "sector"),
        check_vma=False,
    )
```

```python
import functools

import jax
import jax.numpy as jnp
from jax import lax
from jax.experimental import pallas as pl
from jax.experimental.pallas import tpu as pltpu
from jax.sharding import PartitionSpec as P

VMEM_LIMIT = 40 * 1024 * 1024
NP, NR, NB, W = 8, 8, 4, 128
NC = NB * W


def face(a, b, damping, d):
    s = [x + y for x, y in zip(a, b)]
    inv = 1.0 / s[0]
    u = s[1 + d] * inv
    p = 0.4 * (s[4] - 0.5 * (s[1] * s[1] + s[2] * s[2] + s[3] * s[3]) * inv)
    f = [s[1 + d]] + [s[1 + c] * u + p if c == d else s[1 + c] * u for c in range(3)]
    f.append((s[4] + p) * u)
    return [g - damping * (y - x) for g, x, y in zip(f, a, b)]


def pack_edges(q_ref, eddy, h, re_ref, le_ref, rad_ref):
    lane = lax.broadcasted_iota(jnp.int32, (NR, W), 1)

    def plane(p, tiles):
        re, le = tiles
        row, a = p // NP, p % NP
        for f in range(6):
            ref, g = (q_ref, f) if f < 5 else (eddy, 5)
            at = f * 16 + p
            hit = lane == at
            re = jnp.where(hit, pltpu.roll(ref[row, g, a, :, NC - W : NC], lax.rem(at + 1, W), 1), re)
            le = jnp.where(hit, pltpu.roll(ref[row, g, a, :, 0:W], at, 1), le)
            rad_ref[row * 6 + f, pl.ds(a, 1), :] = ref[row, g, a, pl.ds(h, 1), :]
        return re, le

    zero = jnp.zeros((NR, W), jnp.float32)
    re_ref[...], le_ref[...] = lax.fori_loop(0, 2 * NP, plane, (zero, zero))


def pack_faces(q_ref, pm_ref, sm_ref):
    for b in range(NB):
        for c in range(5):
            pm_ref[b * 5 + c] = q_ref[0, c, NP - 1, :, b * W : (b + 1) * W]
            sm_ref[b * 5 + c] = q_ref[1, c, 0, :, b * W : (b + 1) * W]


def faces_kernel(flow_ref, pm_ref, sm_ref, em_ref, q_ref, buf, sem):
    del q_ref
    cps = [
        pltpu.make_async_copy(flow_ref.at[0, :, NP - 1], buf.at[0], sem.at[0]),
        pltpu.make_async_copy(flow_ref.at[1, :, 0], buf.at[1], sem.at[1]),
    ]
    for cp in cps:
        cp.start()
    for cp in cps:
        cp.wait()
    for b in range(NB):
        cells = slice(b * W, (b + 1) * W)
        for c in range(5):
            pm_ref[b * 5 + c] = buf[0, c, :, cells]
            sm_ref[b * 5 + c] = buf[1, c, :, cells]
        em_ref[0, b] = buf[0, 5, :, cells]
        em_ref[1, b] = buf[1, 5, :, cells]


def split(x):
    hi = x.astype(jnp.bfloat16)
    return hi, (x - hi.astype(jnp.float32)).astype(jnp.bfloat16)


def bulk_kernel(sc_ref, span_ref, idx_ref, flow_hbm, q_hbm, w_hbm, out_ref, re_ref, le_ref, rad_ref, wb_ref, wf_ref, inv_ref,
                flow_ref, q_ref, w_ref, acc, sem):
    step, offset = sc_ref[0], sc_ref[1]
    half = jnp.where(step == 0, 0.0625, 0.125)
    get_w = pltpu.make_async_copy(w_hbm.at[step], w_ref, sem.at[0])
    get_flow = pltpu.make_async_copy(flow_hbm, flow_ref, sem.at[1])
    get_w.start()
    get_flow.start()

    @pl.when(step == 0)
    def _():
        cp = pltpu.make_async_copy(flow_hbm.at[:, 0:5], q_ref, sem.at[2])
        cp.start()
        cp.wait()

    @pl.when(step != 0)
    def _():
        cp = pltpu.make_async_copy(q_hbm, q_ref, sem.at[2])
        cp.start()
        cp.wait()

    get_flow.wait()
    lane = lax.broadcasted_iota(jnp.int32, (NR, W), 1)
    sub = lax.broadcasted_iota(jnp.int32, (NR, NC), 0)

    def no_first(g):
        return jnp.concatenate([jnp.where(lane == 0, 0.0, g[:, :W]), g[:, W:]], axis=1)

    for row in range(2):

        def plane(a, below, row=row):
            x = [q_ref[row, f, a] for f in range(5)]
            e = flow_ref[row, 5, a]
            up = jnp.minimum(a + 1, NP - 1)
            above = face(x, [q_ref[row, f, up] for f in range(5)], 0.1 + e + flow_ref[row, 5, up], 2)
            if row == 0:
                keep = jnp.where(a == NP - 1, 0.0, 1.0)
                above = [g * keep for g in above]
            total = [g - l for g, l in zip(above, below)]
            lo = [pltpu.roll(v, 1, 0) for v in x]
            g = face(lo, x, 0.1 + e + pltpu.roll(e, 1, 0), 1)
            g = [jnp.where(sub == 0, 0.0, v) for v in g]
            total = [t + (pltpu.roll(v, NR - 1, 0) - v) for t, v in zip(total, g)]
            lo = [pltpu.roll(v, 1, 1) for v in x]
            g = face(lo, x, 0.1 + e + pltpu.roll(e, 1, 1), 0)
            g = [no_first(v) for v in g]
            total = [t + (pltpu.roll(v, NC - 1, 1) - v) for t, v in zip(total, g)]
            for f in range(5):
                out_ref[row, f, a] = flow_ref[row, f, a] - half * total[f]
            return above

        if row == 0:
            x0 = [q_ref[0, f, 0] for f in range(5)]
            first = face(x0, x0, jnp.zeros((NR, NC), jnp.float32), 2)
        else:
            first = [jnp.zeros((NR, NC), jnp.float32)] * 5
        lax.fori_loop(0, NP, plane, first)

    pack_edges(q_ref, flow_ref, jnp.where(span_ref[0] == 0, NR - 1, 0), re_ref, le_ref, rad_ref)

    get_w.wait()
    acc[...] = jnp.ones(acc.shape, jnp.float32)
    f0 = offset % NB
    for j in range(NB):
        total = jnp.zeros((8, W), jnp.float32)
        for m in range(2):
            w = w_ref[j, m]
            wt = w.T
            wb_ref[0, j, :, m * W : (m + 1) * W], wb_ref[1, j, :, m * W : (m + 1) * W] = split(w)
            wf_ref[0, j, m * W : (m + 1) * W, :], wf_ref[1, j, m * W : (m + 1) * W, :] = split(wt)
            total = total + jnp.sum(wt, axis=0, keepdims=True)
            d = jnp.sum(w, axis=0, keepdims=True)
            b1 = idx_ref[step, j, m] + 3 - f0
            acc[b1] += d
            acc[b1 + 4] += d
        inv_ref[0, j] = 1.0 / total
    for b in range(NB):
        inv_ref[1, b] = 1.0 / acc[NB + b]


def finish_kernel(sc_ref, span_ref, idx_ref, q_hbm, part_ref, pm_ref, sm_ref, em_ref, px_ref, sx_ref, up_ref, down_ref,
                  re_ref, le_ref, rad_ref, radh_ref, wb_ref, wf_ref, inv_ref, out_ref, pm_out, sm_out, win, acc, rfix):
    del q_hbm
    step, offset = sc_ref[0], sc_ref[1]
    half = jnp.where(step == 0, 0.0625, 0.125)
    f0 = offset % NB
    odd = (offset // NB) % 2 == 1
    start = NB - 1 - f0
    nface = 5 * NB
    lower = span_ref[0] == 0
    sgn = jnp.where(lower, 1.0, -1.0)
    h = jnp.where(lower, NR - 1, 0)

    for row in range(2):
        own = [rad_ref[row * 6 + f] for f in range(6)]
        other = [radh_ref[row * 6 + f] for f in range(6)]
        g = face(own[:5], other[:5], sgn * (0.1 + own[5] + other[5]), 1)
        for f in range(5):
            rfix[row * 5 + f] = (-half * sgn) * g[f]

    def both_sides(lo, hi):
        lo, hi = ([t if f == 0 else pltpu.roll(t, W - 16 * f, 1) for f in range(6)] for t in (lo, hi))
        return [half * v for v in face(lo[:5], hi[:5], 0.1 + lo[5] + hi[5], 0)]

    left = both_sides(up_ref[nface], le_ref[...])
    right = both_sides(re_ref[...], down_ref[nface])
    lane = lax.broadcasted_iota(jnp.int32, (NR, W), 1)
    at_h = lax.broadcasted_iota(jnp.int32, (NR, NC), 0) == h

    def plane(p, carry):
        row, a = p // NP, p % NP
        for f in range(5):
            v = part_ref[row, f, a] + jnp.where(at_h, rfix[row * 5 + f, pl.ds(a, 1), :], 0.0)
            lo = jnp.where(lane == 0, pltpu.roll(left[f], lax.rem(W - p, W), 1), 0.0)
            hi = jnp.where(lane == W - 1, pltpu.roll(right[f], W - 1 - p, 1), 0.0)
            out_ref[row, f, a] = jnp.concatenate([v[:, :W] + lo, v[:, W : NC - W], v[:, NC - W :] - hi], axis=1)
        return carry

    lax.fori_loop(0, 2 * NP, plane, 0)

    def dot(x, w_ref, j):
        hi, lo = split(x)
        def one(a, b):
            return jnp.dot(a, b, preferred_element_type=jnp.float32)
        return one(hi, w_ref[0, j]) + (one(hi, w_ref[1, j]) + one(lo, w_ref[0, j]))

    win[NB : 2 * NB] = jnp.where(odd, down_ref[0:nface], px_ref[...]).reshape(NB, 5, NR, W)
    win[0:NB] = jnp.where(odd, px_ref[...], up_ref[0:nface]).reshape(NB, 5, NR, W)
    acc[...] = jnp.zeros(acc.shape, jnp.float32)
    pad = jnp.zeros((8, W), jnp.float32)
    for j in range(NB):
        lhs = jnp.concatenate(
            [jnp.concatenate([win[start + idx_ref[step, j, m]].reshape(40, W), pad], axis=0) for m in range(2)],
            axis=1,
        )
        num = dot(lhs, wf_ref, j)
        inv = inv_ref[0, j]
        ghost = [num[8 * c : 8 * c + 8] * inv for c in range(5)]
        g = face(ghost, [sm_ref[j * 5 + c] for c in range(5)], 0.1 + 2.0 * em_ref[1, j], 2)
        for c in range(5):
            cells = (1, c, 0, slice(None), slice(j * W, (j + 1) * W))
            out_ref[cells] = out_ref[cells] + half * g[c]
        blk = slice(j * 5, j * 5 + 5)
        s1 = jnp.where(odd, up_ref[blk], sx_ref[blk]).reshape(40, W)
        s2 = jnp.where(odd, sx_ref[blk], down_ref[blk]).reshape(40, W)
        r = dot(jnp.concatenate([s1, s2], axis=0), wb_ref, j)
        for m in range(2):
            b1 = idx_ref[step, j, m] + 3 - f0
            acc[b1] += r[0:40, m * W : (m + 1) * W]
            acc[b1 + 4] += r[40:80, m * W : (m + 1) * W]
    for b in range(NB):
        inv = inv_ref[1, b]
        own = [pm_ref[b * 5 + c] for c in range(5)]
        ghost = [(acc[NB + b, 8 * c : 8 * c + 8] + own[c]) * inv for c in range(5)]
        g = face(own, ghost, 0.1 + 2.0 * em_ref[0, b], 2)
        for c in range(5):
            cells = (0, c, NP - 1, slice(None), slice(b * W, (b + 1) * W))
            out_ref[cells] = out_ref[cells] - half * g[c]
    pack_faces(out_ref, pm_out, sm_out)


SMEM = pl.BlockSpec(memory_space=pltpu.SMEM)
VMEM = pl.BlockSpec(memory_space=pltpu.VMEM)
ANY = pl.BlockSpec(memory_space=pl.ANY)
PARAMS = pltpu.CompilerParams(vmem_limit_bytes=VMEM_LIMIT)


def arr(*shape, dtype=jnp.float32):
    return jax.ShapeDtypeStruct(shape, dtype)


def buffer(*shape):
    return pltpu.VMEM(shape, jnp.float32)


FACE = (NB * 5, NR, W)
TILE = (NR, W)
STATE = (2, 5, NP, NR, NC)
HALVES = (2, NB, W, 2 * W)
HALVES_T = (2, NB, 2 * W, W)


def perm(x, d):
    n = lax.axis_size("sector")
    return lax.ppermute(x, "sector", [(i, (i + d) % n) for i in range(n)])


def both(d):
    if d == 0:
        return lambda p, s: (p, s)
    return lambda p, s: (perm(p, d), perm(s, -d))


def bulk(sc, span, intersections, flow, q, weights):
    return pl.pallas_call(
        bulk_kernel,
        in_specs=[SMEM] * 3 + [ANY] * 3,
        out_specs=[VMEM] * 7,
        out_shape=[
            arr(*STATE), arr(*TILE), arr(*TILE), arr(12, NP, NC),
            arr(*HALVES, dtype=jnp.bfloat16), arr(*HALVES_T, dtype=jnp.bfloat16), arr(2, NB, NR, W),
        ],
        scratch_shapes=[
            buffer(2, 6, NP, NR, NC), buffer(*STATE), buffer(NB, 2, W, W), buffer(3 * NB, NR, W), pltpu.SemaphoreType.DMA((3,)),
        ],
        compiler_params=PARAMS,
        cost_estimate=pl.CostEstimate(flops=20_000_000, bytes_accessed=8_000_000, transcendentals=0),
        name="bulk",
    )(sc, span, intersections, flow, q, weights)


def local(flow, offsets, intersections, weights):
    span = lax.axis_index("span").astype(jnp.int32).reshape(1)
    pm, sm, em, q = pl.pallas_call(
        faces_kernel,
        in_specs=[ANY],
        out_specs=[VMEM] * 3 + [ANY],
        out_shape=[arr(*FACE), arr(*FACE), arr(2, NB, NR, W), arr(*STATE)],
        scratch_shapes=[buffer(2, 6, NR, NC), pltpu.SemaphoreType.DMA((2,))],
        compiler_params=PARAMS,
        name="faces",
    )(flow)

    def section(step, carry):
        offset, following, q, pm, sm = carry
        k = offset // NB
        odd = (k & 1) == 1
        even = (k + 1) >> 1
        sc = jnp.stack([step, offset])
        p, s = lax.switch(even & 7, [both(2 * i) for i in range(8)], pm, sm)

        def leaf(d):
            return lambda p, s, *rest: both(d)(p, s) + tuple(bulk(*rest))

        px, sx, part, re, le, rad, wb, wf, inv = lax.switch(
            (even >> 3) & 7, [leaf(16 * i) for i in range(8)], p, s, sc, span, intersections, flow, q, weights
        )
        up = perm(jnp.concatenate([jnp.where(odd, sx, px), re[None]]), 1)
        down = perm(jnp.concatenate([jnp.where(odd, px, sx), le[None]]), -1)
        radh = lax.ppermute(rad, "span", [(0, 1), (1, 0)])
        q, pm, sm = pl.pallas_call(
            finish_kernel,
            in_specs=[SMEM] * 3 + [ANY] + [VMEM] * 15,
            out_specs=[VMEM] * 3,
            out_shape=[arr(*STATE), arr(*FACE), arr(*FACE)],
            scratch_shapes=[buffer(2 * NB, 5, NR, W), buffer(3 * NB, 40, W), buffer(10, NP, NC)],
            input_output_aliases={3: 0, 5: 1, 6: 2},
            compiler_params=PARAMS,
            name="finish",
        )(sc, span, intersections, q, part, pm, sm, em, px, sx, up, down, re, le, rad, radh, wb, wf, inv)
        return following, following, q, pm, sm

    return lax.fori_loop(0, 2, section, (offsets[0], offsets[1], q, pm, sm))[2]


def solution(mesh):
    return jax.shard_map(
        local,
        mesh=mesh,
        in_specs=(P(None, None, None, "span", "sector"), P(), P(), P()),
        out_specs=P(None, None, None, "span", "sector"),
        check_vma=False,
    )
```

```python
import functools

import jax
import jax.numpy as jnp
from jax import lax
from jax.experimental import pallas as pl
from jax.experimental.pallas import tpu as pltpu
from jax.sharding import PartitionSpec as P

VMEM_LIMIT = 24 * 1024 * 1024
NP, NR, NB, W = 8, 8, 4, 128
NC = NB * W


def face(a, b, damping, d):
    s = [x + y for x, y in zip(a, b)]
    inv = 1.0 / s[0]
    u = s[1 + d] * inv
    p = 0.4 * (s[4] - 0.5 * (s[1] * s[1] + s[2] * s[2] + s[3] * s[3]) * inv)
    f = [s[1 + d]] + [s[1 + c] * u + p if c == d else s[1 + c] * u for c in range(3)]
    f.append((s[4] + p) * u)
    return [g - damping * (y - x) for g, x, y in zip(f, a, b)]


def pack_edges(q_ref, eddy, h, re_ref, le_ref, rad_ref):
    lane = lax.broadcasted_iota(jnp.int32, (NR, W), 1)

    def plane(p, tiles):
        re, le = tiles
        row, a = p // NP, p % NP
        for f in range(6):
            ref, g = (q_ref, f) if f < 5 else (eddy, 5)
            at = f * 16 + p
            hit = lane == at
            re = jnp.where(hit, pltpu.roll(ref[row, g, a, :, NC - W : NC], lax.rem(at + 1, W), 1), re)
            le = jnp.where(hit, pltpu.roll(ref[row, g, a, :, 0:W], at, 1), le)
            rad_ref[row * 6 + f, pl.ds(a, 1), :] = ref[row, g, a, pl.ds(h, 1), :]
        return re, le

    zero = jnp.zeros((NR, W), jnp.float32)
    re_ref[...], le_ref[...] = lax.fori_loop(0, 2 * NP, plane, (zero, zero))


def pack_faces(q_ref, pm_ref, sm_ref):
    for b in range(NB):
        for c in range(5):
            pm_ref[b * 5 + c] = q_ref[0, c, NP - 1, :, b * W : (b + 1) * W]
            sm_ref[b * 5 + c] = q_ref[1, c, 0, :, b * W : (b + 1) * W]


def faces_kernel(off_ref, flow_ref, pm_ref, sm_ref, em_ref, q_ref, *rest):
    digits, (buf, sem) = rest[:4], rest[4:]
    cps = [
        pltpu.make_async_copy(flow_ref.at[0, :, NP - 1], buf.at[0], sem.at[0]),
        pltpu.make_async_copy(flow_ref.at[1, :, 0], buf.at[1], sem.at[1]),
        pltpu.make_async_copy(flow_ref.at[:, 0:5], q_ref, sem.at[2]),
    ]
    for cp in cps:
        cp.start()
    for step in range(2):
        even = (off_ref[step] // NB + 1) >> 1
        digits[2 * step][0] = even & 7
        digits[2 * step + 1][0] = (even >> 3) & 7
    for cp in cps[:2]:
        cp.wait()
    for b in range(NB):
        cells = slice(b * W, (b + 1) * W)
        for c in range(5):
            pm_ref[b * 5 + c] = buf[0, c, :, cells]
            sm_ref[b * 5 + c] = buf[1, c, :, cells]
        em_ref[0, b] = buf[0, 5, :, cells]
        em_ref[1, b] = buf[1, 5, :, cells]
    cps[2].wait()


def split(x):
    hi = x.astype(jnp.bfloat16)
    return hi, (x - hi.astype(jnp.float32)).astype(jnp.bfloat16)


def bulk_kernel(step_ref, flow_ref, q_ref, out_ref):
    half = jnp.where(step_ref[0] == 0, 0.0625, 0.125)
    lane = lax.broadcasted_iota(jnp.int32, (NR, W), 1)
    sub = lax.broadcasted_iota(jnp.int32, (NR, NC), 0)

    def no_first(g):
        return jnp.concatenate([jnp.where(lane == 0, 0.0, g[:, :W]), g[:, W:]], axis=1)

    for row in range(2):

        def plane(a, below, row=row):
            x = [q_ref[row, f, a] for f in range(5)]
            e = flow_ref[row, 5, a]
            up = jnp.minimum(a + 1, NP - 1)
            above = face(x, [q_ref[row, f, up] for f in range(5)], 0.1 + e + flow_ref[row, 5, up], 2)
            if row == 0:
                keep = jnp.where(a == NP - 1, 0.0, 1.0)
                above = [g * keep for g in above]
            total = [g - l for g, l in zip(above, below)]
            lo = [pltpu.roll(v, 1, 0) for v in x]
            g = face(lo, x, 0.1 + e + pltpu.roll(e, 1, 0), 1)
            g = [jnp.where(sub == 0, 0.0, v) for v in g]
            total = [t + (pltpu.roll(v, NR - 1, 0) - v) for t, v in zip(total, g)]
            lo = [pltpu.roll(v, 1, 1) for v in x]
            g = face(lo, x, 0.1 + e + pltpu.roll(e, 1, 1), 0)
            g = [no_first(v) for v in g]
            total = [t + (pltpu.roll(v, NC - 1, 1) - v) for t, v in zip(total, g)]
            for f in range(5):
                out_ref[row, f, a] = flow_ref[row, f, a] - half * total[f]
            return above

        if row == 0:
            x0 = [q_ref[0, f, 0] for f in range(5)]
            first = face(x0, x0, jnp.zeros((NR, NC), jnp.float32), 2)
        else:
            first = [jnp.zeros((NR, NC), jnp.float32)] * 5
        lax.fori_loop(0, NP, plane, first)


def prep_kernel(step_ref, off_ref, span_ref, idx_ref, flow_ref, q_ref, w_hbm, re_ref, le_ref, rad_ref, wb_ref, wf_ref, inv_ref,
                w_ref, acc, sem):
    step, offset = step_ref[0], off_ref[0]
    get_w = pltpu.make_async_copy(w_hbm.at[step], w_ref, sem)
    get_w.start()
    pack_edges(q_ref, flow_ref, jnp.where(span_ref[0] == 0, NR - 1, 0), re_ref, le_ref, rad_ref)

    get_w.wait()
    acc[...] = jnp.ones(acc.shape, jnp.float32)
    f0 = offset % NB
    for j in range(NB):
        total = jnp.zeros((8, W), jnp.float32)
        for m in range(2):
            w = w_ref[j, m]
            wt = w.T
            wb_ref[0, j, :, m * W : (m + 1) * W], wb_ref[1, j, :, m * W : (m + 1) * W] = split(w)
            wf_ref[0, j, m * W : (m + 1) * W, :], wf_ref[1, j, m * W : (m + 1) * W, :] = split(wt)
            total = total + jnp.sum(wt, axis=0, keepdims=True)
            d = jnp.sum(w, axis=0, keepdims=True)
            b1 = idx_ref[step, j, m] + 3 - f0
            acc[b1] += d
            acc[b1 + 4] += d
        inv_ref[0, j] = 1.0 / total
    for b in range(NB):
        inv_ref[1, b] = 1.0 / acc[NB + b]


def join_kernel(off_ref, p_ref, s_ref, re_ref, le_ref, up_ref, down_ref):
    n = 5 * NB
    odd = (off_ref[0] // NB) % 2 == 1
    up_ref[n] = re_ref[...]
    down_ref[n] = le_ref[...]
    for i in range(n):
        up_ref[i] = jnp.where(odd, s_ref[i], p_ref[i])
        down_ref[i] = jnp.where(odd, p_ref[i], s_ref[i])


def finish_kernel(step_ref, off_ref, span_ref, idx_ref, q_hbm, part_ref, pm_ref, sm_ref, em_ref, mu_ref, md_ref, up_ref, down_ref,
                  re_ref, le_ref, rad_ref, radh_ref, wb_ref, wf_ref, inv_ref, out_ref, pm_out, sm_out, win, acc, rfix):
    del q_hbm
    step, offset = step_ref[0], off_ref[0]
    half = jnp.where(step == 0, 0.0625, 0.125)
    f0 = offset % NB
    odd = (offset // NB) % 2 == 1
    start = NB - 1 - f0
    nface = 5 * NB
    lower = span_ref[0] == 0
    sgn = jnp.where(lower, 1.0, -1.0)
    h = jnp.where(lower, NR - 1, 0)

    for row in range(2):
        own = [rad_ref[row * 6 + f] for f in range(6)]
        other = [radh_ref[row * 6 + f] for f in range(6)]
        g = face(own[:5], other[:5], sgn * (0.1 + own[5] + other[5]), 1)
        for f in range(5):
            rfix[row * 5 + f] = (-half * sgn) * g[f]

    def both_sides(lo, hi):
        lo, hi = ([t if f == 0 else pltpu.roll(t, W - 16 * f, 1) for f in range(6)] for t in (lo, hi))
        return [half * v for v in face(lo[:5], hi[:5], 0.1 + lo[5] + hi[5], 0)]

    left = both_sides(up_ref[nface], le_ref[...])
    right = both_sides(re_ref[...], down_ref[nface])
    lane = lax.broadcasted_iota(jnp.int32, (NR, W), 1)
    at_h = lax.broadcasted_iota(jnp.int32, (NR, NC), 0) == h

    def plane(p, carry):
        row, a = p // NP, p % NP
        for f in range(5):
            v = part_ref[row, f, a] + jnp.where(at_h, rfix[row * 5 + f, pl.ds(a, 1), :], 0.0)
            lo = jnp.where(lane == 0, pltpu.roll(left[f], lax.rem(W - p, W), 1), 0.0)
            hi = jnp.where(lane == W - 1, pltpu.roll(right[f], W - 1 - p, 1), 0.0)
            out_ref[row, f, a] = jnp.concatenate([v[:, :W] + lo, v[:, W : NC - W], v[:, NC - W :] - hi], axis=1)
        return carry

    lax.fori_loop(0, 2 * NP, plane, 0)

    def dot(x, w_ref, j):
        hi, lo = split(x)
        def one(a, b):
            return jnp.dot(a, b, preferred_element_type=jnp.float32)
        return one(hi, w_ref[0, j]) + (one(hi, w_ref[1, j]) + one(lo, w_ref[0, j]))

    win[NB : 2 * NB] = jnp.where(odd, down_ref[0:nface], mu_ref[0:nface]).reshape(NB, 5, NR, W)
    win[0:NB] = jnp.where(odd, md_ref[0:nface], up_ref[0:nface]).reshape(NB, 5, NR, W)
    acc[...] = jnp.zeros(acc.shape, jnp.float32)
    pad = jnp.zeros((8, W), jnp.float32)
    for j in range(NB):
        lhs = jnp.concatenate(
            [jnp.concatenate([win[start + idx_ref[step, j, m]].reshape(40, W), pad], axis=0) for m in range(2)],
            axis=1,
        )
        num = dot(lhs, wf_ref, j)
        inv = inv_ref[0, j]
        ghost = [num[8 * c : 8 * c + 8] * inv for c in range(5)]
        g = face(ghost, [sm_ref[j * 5 + c] for c in range(5)], 0.1 + 2.0 * em_ref[1, j], 2)
        for c in range(5):
            cells = (1, c, 0, slice(None), slice(j * W, (j + 1) * W))
            out_ref[cells] = out_ref[cells] + half * g[c]
        blk = slice(j * 5, j * 5 + 5)
        s1 = jnp.where(odd, up_ref[blk], md_ref[blk]).reshape(40, W)
        s2 = jnp.where(odd, mu_ref[blk], down_ref[blk]).reshape(40, W)
        r = dot(jnp.concatenate([s1, s2], axis=0), wb_ref, j)
        for m in range(2):
            b1 = idx_ref[step, j, m] + 3 - f0
            acc[b1] += r[0:40, m * W : (m + 1) * W]
            acc[b1 + 4] += r[40:80, m * W : (m + 1) * W]
    for b in range(NB):
        inv = inv_ref[1, b]
        own = [pm_ref[b * 5 + c] for c in range(5)]
        ghost = [(acc[NB + b, 8 * c : 8 * c + 8] + own[c]) * inv for c in range(5)]
        g = face(own, ghost, 0.1 + 2.0 * em_ref[0, b], 2)
        for c in range(5):
            cells = (0, c, NP - 1, slice(None), slice(b * W, (b + 1) * W))
            out_ref[cells] = out_ref[cells] - half * g[c]
    pack_faces(out_ref, pm_out, sm_out)


SMEM = pl.BlockSpec(memory_space=pltpu.SMEM)
VMEM = pl.BlockSpec(memory_space=pltpu.VMEM)
ANY = pl.BlockSpec(memory_space=pl.ANY)
PARAMS = pltpu.CompilerParams(vmem_limit_bytes=VMEM_LIMIT)


def arr(*shape, dtype=jnp.float32):
    return jax.ShapeDtypeStruct(shape, dtype)


def buffer(*shape):
    return pltpu.VMEM(shape, jnp.float32)


FACE = (NB * 5, NR, W)
TILE = (NR, W)
STATE = (2, 5, NP, NR, NC)
HALVES = (2, NB, W, 2 * W)
HALVES_T = (2, NB, 2 * W, W)


def perm(x, d):
    n = lax.axis_size("sector")
    return lax.ppermute(x, "sector", [(i, (i + d) % n) for i in range(n)])


def both(d):
    if d == 0:
        return lambda p, s: (p, s)
    return lambda p, s: (perm(p, d), perm(s, -d))


def call(kernel, name, in_specs, out_shape, operands, scratch=(), **kw):
    return pl.pallas_call(
        kernel,
        in_specs=in_specs,
        out_specs=[VMEM] * len(out_shape),
        out_shape=out_shape,
        scratch_shapes=list(scratch),
        compiler_params=PARAMS,
        name=name,
        **kw,
    )(*operands)


def prep(*operands):
    return call(
        prep_kernel, "prep", [SMEM] * 4 + [VMEM] * 2 + [ANY],
        [
            arr(*TILE), arr(*TILE), arr(12, NP, NC),
            arr(*HALVES, dtype=jnp.bfloat16), arr(*HALVES_T, dtype=jnp.bfloat16), arr(2, NB, NR, W),
        ],
        operands,
        [buffer(NB, 2, W, W), buffer(3 * NB, NR, W), pltpu.SemaphoreType.DMA],
        cost_estimate=pl.CostEstimate(flops=10_000_000, bytes_accessed=4_000_000, transcendentals=0),
    )


def bulk(*operands):
    return call(
        bulk_kernel, "bulk", [SMEM] + [VMEM] * 2, [arr(*STATE)], operands,
        cost_estimate=pl.CostEstimate(flops=20_000_000, bytes_accessed=8_000_000, transcendentals=0),
    )[0]


def local(flow, offsets, intersections, weights):
    span = lax.axis_index("span").astype(jnp.int32).reshape(1)
    one = jax.ShapeDtypeStruct((1,), jnp.int32)
    pm, sm, em, q, *digits = pl.pallas_call(
        faces_kernel,
        in_specs=[SMEM, ANY],
        out_specs=[VMEM] * 4 + [SMEM] * 4,
        out_shape=[arr(*FACE), arr(*FACE), arr(2, NB, NR, W), arr(*STATE)] + [one] * 4,
        scratch_shapes=[buffer(2, 6, NR, NC), pltpu.SemaphoreType.DMA((3,))],
        compiler_params=PARAMS,
        name="faces",
    )(offsets, flow)
    digits = [d.reshape(()) for d in digits]

    def section(step, carry):
        offset, now, following, then, q, pm, sm = carry
        at = step.reshape(1), offset

        def first(d):
            def run(p, s, *rest):
                return both(d)(p, s) + tuple(prep(*rest))
            return run

        p, s, re, le, rad, wb, wf, inv = lax.switch(
            now[0], [first(2 * i) for i in range(8)], pm, sm, *at, span, intersections, flow, q, weights
        )
        radh = lax.ppermute(rad, "span", [(0, 1), (1, 0)])

        def second(d):
            def run(p, s, step, offset, flow, q, re, le):
                p, s = both(d)(p, s)
                part = bulk(step, flow, q)
                msgs = [arr(NB * 5 + 1, NR, W)] * 2
                return (*call(join_kernel, "join", [SMEM] + [VMEM] * 4, msgs, (offset, p, s, re, le)), part)
            return run

        mu, md, part = lax.switch(now[1], [second(16 * i) for i in range(8)], p, s, *at, flow, q, re, le)
        up, down = perm(mu, 1), perm(md, -1)
        q, pm, sm = call(
            finish_kernel, "finish", [SMEM] * 4 + [ANY] + [VMEM] * 15, [arr(*STATE), arr(*FACE), arr(*FACE)],
            (*at, span, intersections, q, part, pm, sm, em, mu, md, up, down, re, le, rad, radh, wb, wf, inv),
            [buffer(2 * NB, 5, NR, W), buffer(3 * NB, 40, W), buffer(10, NP, NC)],
            input_output_aliases={4: 0, 6: 1, 7: 2},
        )
        return following, then, following, then, q, pm, sm

    carry = (offsets[0:1], tuple(digits[:2]), offsets[1:2], tuple(digits[2:]), q, pm, sm)
    return lax.fori_loop(0, 2, section, carry)[4]


def solution(mesh):
    return jax.shard_map(
        local,
        mesh=mesh,
        in_specs=(P(None, None, None, "span", "sector"), P(), P(), P()),
        out_specs=P(None, None, None, "span", "sector"),
        check_vma=False,
    )
```

```python
import functools

import jax
import jax.numpy as jnp
from jax import lax
from jax.experimental import pallas as pl
from jax.experimental.pallas import tpu as pltpu
from jax.sharding import PartitionSpec as P

VMEM_LIMIT = 24 * 1024 * 1024
NP, NR, NB, W = 8, 8, 4, 128
NC = NB * W


def face(a, b, damping, d):
    s = [x + y for x, y in zip(a, b)]
    inv = 1.0 / s[0]
    u = s[1 + d] * inv
    p = 0.4 * (s[4] - 0.5 * (s[1] * s[1] + s[2] * s[2] + s[3] * s[3]) * inv)
    f = [s[1 + d]] + [s[1 + c] * u + p if c == d else s[1 + c] * u for c in range(3)]
    f.append((s[4] + p) * u)
    return [g - damping * (y - x) for g, x, y in zip(f, a, b)]


def pack_edges(first, flow_ref, q_ref, h, re_ref, le_ref, rad_ref):
    lane = lax.broadcasted_iota(jnp.int32, (NR, W), 1)

    def plane(p, tiles):
        re, le = tiles
        row, a = p // NP, p % NP
        for f in range(6):
            def get(r, c, f=f):
                x = flow_ref[row, f, a, r, c]
                return x if f == 5 else jnp.where(first, x, q_ref[row, f, a, r, c])
            at = f * 16 + p
            hit = lane == at
            re = jnp.where(hit, pltpu.roll(get(slice(None), slice(NC - W, NC)), lax.rem(at + 1, W), 1), re)
            le = jnp.where(hit, pltpu.roll(get(slice(None), slice(0, W)), at, 1), le)
            rad_ref[row * 6 + f, pl.ds(a, 1), :] = get(pl.ds(h, 1), slice(None))
        return re, le

    zero = jnp.zeros((NR, W), jnp.float32)
    re_ref[...], le_ref[...] = lax.fori_loop(0, 2 * NP, plane, (zero, zero))


def pack_faces(q_ref, pm_ref, sm_ref):
    for b in range(NB):
        for c in range(5):
            pm_ref[b * 5 + c] = q_ref[0, c, NP - 1, :, b * W : (b + 1) * W]
            sm_ref[b * 5 + c] = q_ref[1, c, 0, :, b * W : (b + 1) * W]


def faces_kernel(off_ref, flow_ref, pm_ref, sm_ref, em_ref, q_ref, *rest):
    del q_ref
    digits, (buf, sem) = rest[:4], rest[4:]
    cps = [
        pltpu.make_async_copy(flow_ref.at[0, :, NP - 1], buf.at[0], sem.at[0]),
        pltpu.make_async_copy(flow_ref.at[1, :, 0], buf.at[1], sem.at[1]),
    ]
    for cp in cps:
        cp.start()
    for step in range(2):
        even = (off_ref[step] // NB + 1) >> 1
        digits[2 * step][0] = even & 7
        digits[2 * step + 1][0] = (even >> 3) & 7
    for cp in cps:
        cp.wait()
    for b in range(NB):
        cells = slice(b * W, (b + 1) * W)
        for c in range(5):
            pm_ref[b * 5 + c] = buf[0, c, :, cells]
            sm_ref[b * 5 + c] = buf[1, c, :, cells]
        em_ref[0, b] = buf[0, 5, :, cells]
        em_ref[1, b] = buf[1, 5, :, cells]


def split(x):
    hi = x.astype(jnp.bfloat16)
    return hi, (x - hi.astype(jnp.float32)).astype(jnp.bfloat16)


def bulk_kernel(step_ref, flow_ref, q_ref, out_ref):
    first_section = step_ref[0] == 0
    half = jnp.where(first_section, 0.0625, 0.125)
    lane = lax.broadcasted_iota(jnp.int32, (NR, W), 1)
    sub = lax.broadcasted_iota(jnp.int32, (NR, NC), 0)

    def no_first(g):
        return jnp.concatenate([jnp.where(lane == 0, 0.0, g[:, :W]), g[:, W:]], axis=1)

    def cells(row, a):
        return [jnp.where(first_section, flow_ref[row, f, a], q_ref[row, f, a]) for f in range(5)]

    for row in range(2):

        def plane(a, carry, row=row):
            x, below = carry
            e = flow_ref[row, 5, a]
            up = jnp.minimum(a + 1, NP - 1)
            following = cells(row, up)
            above = face(x, following, 0.1 + e + flow_ref[row, 5, up], 2)
            if row == 0:
                keep = jnp.where(a == NP - 1, 0.0, 1.0)
                above = [g * keep for g in above]
            total = [g - l for g, l in zip(above, below)]
            lo = [pltpu.roll(v, 1, 0) for v in x]
            g = face(lo, x, 0.1 + e + pltpu.roll(e, 1, 0), 1)
            g = [jnp.where(sub == 0, 0.0, v) for v in g]
            total = [t + (pltpu.roll(v, NR - 1, 0) - v) for t, v in zip(total, g)]
            lo = [pltpu.roll(v, 1, 1) for v in x]
            g = face(lo, x, 0.1 + e + pltpu.roll(e, 1, 1), 0)
            g = [no_first(v) for v in g]
            total = [t + (pltpu.roll(v, NC - 1, 1) - v) for t, v in zip(total, g)]
            for f in range(5):
                out_ref[row, f, a] = flow_ref[row, f, a] - half * total[f]
            return following, above

        x0 = cells(row, 0)
        if row == 0:
            below = face(x0, x0, jnp.zeros((NR, NC), jnp.float32), 2)
        else:
            below = [jnp.zeros((NR, NC), jnp.float32)] * 5
        lax.fori_loop(0, NP, plane, (x0, below))


def prep_kernel(step_ref, off_ref, span_ref, idx_ref, flow_ref, q_ref, w_hbm, re_ref, le_ref, rad_ref, wb_ref, wf_ref, inv_ref,
                w_ref, acc, sem):
    step = step_ref[0]
    offset = off_ref[step]
    get_w = pltpu.make_async_copy(w_hbm.at[step], w_ref, sem)
    get_w.start()
    pack_edges(step == 0, flow_ref, q_ref, jnp.where(span_ref[0] == 0, NR - 1, 0), re_ref, le_ref, rad_ref)

    get_w.wait()
    acc[...] = jnp.ones(acc.shape, jnp.float32)
    f0 = offset % NB
    for j in range(NB):
        total = jnp.zeros((8, W), jnp.float32)
        for m in range(2):
            w = w_ref[j, m]
            wt = w.T
            wb_ref[0, j, :, m * W : (m + 1) * W], wb_ref[1, j, :, m * W : (m + 1) * W] = split(w)
            wf_ref[0, j, m * W : (m + 1) * W, :], wf_ref[1, j, m * W : (m + 1) * W, :] = split(wt)
            total = total + jnp.sum(wt, axis=0, keepdims=True)
            d = jnp.sum(w, axis=0, keepdims=True)
            b1 = idx_ref[step, j, m] + 3 - f0
            acc[b1] += d
            acc[b1 + 4] += d
        inv_ref[0, j] = 1.0 / total
    for b in range(NB):
        inv_ref[1, b] = 1.0 / acc[NB + b]


def join_kernel(step_ref, off_ref, p_ref, s_ref, re_ref, le_ref, up_ref, down_ref):
    n = 5 * NB
    odd = (off_ref[step_ref[0]] // NB) % 2 == 1
    up_ref[n] = re_ref[...]
    down_ref[n] = le_ref[...]
    for i in range(n):
        up_ref[i] = jnp.where(odd, s_ref[i], p_ref[i])
        down_ref[i] = jnp.where(odd, p_ref[i], s_ref[i])


def radial_kernel(step_ref, span_ref, part_ref, rad_ref, radh_ref, out_ref, rfix):
    half = jnp.where(step_ref[0] == 0, 0.0625, 0.125)
    lower = span_ref[0] == 0
    sgn = jnp.where(lower, 1.0, -1.0)
    at_h = lax.broadcasted_iota(jnp.int32, (NR, NC), 0) == jnp.where(lower, NR - 1, 0)
    for row in range(2):
        own = [rad_ref[row * 6 + f] for f in range(6)]
        other = [radh_ref[row * 6 + f] for f in range(6)]
        g = face(own[:5], other[:5], sgn * (0.1 + own[5] + other[5]), 1)
        for f in range(5):
            rfix[row * 5 + f] = (-half * sgn) * g[f]

    def plane(p, carry):
        row, a = p // NP, p % NP
        for f in range(5):
            out_ref[row, f, a] = part_ref[row, f, a] + jnp.where(at_h, rfix[row * 5 + f, pl.ds(a, 1), :], 0.0)
        return carry

    lax.fori_loop(0, 2 * NP, plane, 0)


def finish_kernel(step_ref, off_ref, idx_ref, q_hbm, part_ref, pm_ref, sm_ref, em_ref, mu_ref, md_ref, up_ref, down_ref,
                  re_ref, le_ref, wb_ref, wf_ref, inv_ref, out_ref, pm_out, sm_out, win, acc):
    del q_hbm
    step = step_ref[0]
    offset = off_ref[step]
    half = jnp.where(step == 0, 0.0625, 0.125)
    f0 = offset % NB
    odd = (offset // NB) % 2 == 1
    start = NB - 1 - f0
    nface = 5 * NB

    def both_sides(lo, hi):
        lo, hi = ([t if f == 0 else pltpu.roll(t, W - 16 * f, 1) for f in range(6)] for t in (lo, hi))
        return [half * v for v in face(lo[:5], hi[:5], 0.1 + lo[5] + hi[5], 0)]

    left = both_sides(up_ref[nface], le_ref[...])
    right = both_sides(re_ref[...], down_ref[nface])
    lane = lax.broadcasted_iota(jnp.int32, (NR, W), 1)
    for row in range(2):
        for a in range(NP):
            p = row * NP + a
            for f in range(5):
                lo = jnp.where(lane == 0, pltpu.roll(left[f], (W - p) % W, 1), 0.0)
                hi = jnp.where(lane == W - 1, pltpu.roll(right[f], W - 1 - p, 1), 0.0)
                out_ref[row, f, a, :, 0:W] = part_ref[row, f, a, :, 0:W] + lo
                out_ref[row, f, a, :, W : NC - W] = part_ref[row, f, a, :, W : NC - W]
                out_ref[row, f, a, :, NC - W : NC] = part_ref[row, f, a, :, NC - W : NC] - hi

    def dot(x, w_ref, j):
        hi, lo = split(x)
        def one(a, b):
            return jnp.dot(a, b, preferred_element_type=jnp.float32)
        return one(hi, w_ref[0, j]) + (one(hi, w_ref[1, j]) + one(lo, w_ref[0, j]))

    win[NB : 2 * NB] = jnp.where(odd, down_ref[0:nface], mu_ref[0:nface]).reshape(NB, 5, NR, W)
    win[0:NB] = jnp.where(odd, md_ref[0:nface], up_ref[0:nface]).reshape(NB, 5, NR, W)
    acc[...] = jnp.zeros(acc.shape, jnp.float32)
    pad = jnp.zeros((8, W), jnp.float32)
    for j in range(NB):
        lhs = jnp.concatenate(
            [jnp.concatenate([win[start + idx_ref[step, j, m]].reshape(40, W), pad], axis=0) for m in range(2)],
            axis=1,
        )
        num = dot(lhs, wf_ref, j)
        inv = inv_ref[0, j]
        ghost = [num[8 * c : 8 * c + 8] * inv for c in range(5)]
        g = face(ghost, [sm_ref[j * 5 + c] for c in range(5)], 0.1 + 2.0 * em_ref[1, j], 2)
        for c in range(5):
            cells = (1, c, 0, slice(None), slice(j * W, (j + 1) * W))
            out_ref[cells] = out_ref[cells] + half * g[c]
        blk = slice(j * 5, j * 5 + 5)
        s1 = jnp.where(odd, up_ref[blk], md_ref[blk]).reshape(40, W)
        s2 = jnp.where(odd, mu_ref[blk], down_ref[blk]).reshape(40, W)
        r = dot(jnp.concatenate([s1, s2], axis=0), wb_ref, j)
        for m in range(2):
            b1 = idx_ref[step, j, m] + 3 - f0
            acc[b1] += r[0:40, m * W : (m + 1) * W]
            acc[b1 + 4] += r[40:80, m * W : (m + 1) * W]
    for b in range(NB):
        inv = inv_ref[1, b]
        own = [pm_ref[b * 5 + c] for c in range(5)]
        ghost = [(acc[NB + b, 8 * c : 8 * c + 8] + own[c]) * inv for c in range(5)]
        g = face(own, ghost, 0.1 + 2.0 * em_ref[0, b], 2)
        for c in range(5):
            cells = (0, c, NP - 1, slice(None), slice(b * W, (b + 1) * W))
            out_ref[cells] = out_ref[cells] - half * g[c]
    pack_faces(out_ref, pm_out, sm_out)


SMEM = pl.BlockSpec(memory_space=pltpu.SMEM)
VMEM = pl.BlockSpec(memory_space=pltpu.VMEM)
ANY = pl.BlockSpec(memory_space=pl.ANY)
PARAMS = pltpu.CompilerParams(vmem_limit_bytes=VMEM_LIMIT)


def arr(*shape, dtype=jnp.float32):
    return jax.ShapeDtypeStruct(shape, dtype)


def buffer(*shape):
    return pltpu.VMEM(shape, jnp.float32)


FACE = (NB * 5, NR, W)
TILE = (NR, W)
STATE = (2, 5, NP, NR, NC)
HALVES = (2, NB, W, 2 * W)
HALVES_T = (2, NB, 2 * W, W)


def perm(x, d):
    n = lax.axis_size("sector")
    return lax.ppermute(x, "sector", [(i, (i + d) % n) for i in range(n)])


def both(d):
    if d == 0:
        return lambda p, s: (p, s)
    return lambda p, s: (perm(p, d), perm(s, -d))


def call(kernel, name, in_specs, out_shape, operands, scratch=(), out_specs=None, **kw):
    return pl.pallas_call(
        kernel,
        in_specs=in_specs,
        out_specs=out_specs or [VMEM] * len(out_shape),
        out_shape=out_shape,
        scratch_shapes=list(scratch),
        compiler_params=PARAMS,
        name=name,
        **kw,
    )(*operands)


def prep(*operands):
    return call(
        prep_kernel, "prep", [SMEM] * 4 + [VMEM] * 2 + [ANY],
        [
            arr(*TILE), arr(*TILE), arr(12, NP, NC),
            arr(*HALVES, dtype=jnp.bfloat16), arr(*HALVES_T, dtype=jnp.bfloat16), arr(2, NB, NR, W),
        ],
        operands,
        [buffer(NB, 2, W, W), buffer(3 * NB, NR, W), pltpu.SemaphoreType.DMA],
        cost_estimate=pl.CostEstimate(flops=10_000_000, bytes_accessed=4_000_000, transcendentals=0),
    )


def bulk(*operands):
    return call(
        bulk_kernel, "bulk", [SMEM] + [VMEM] * 2, [arr(*STATE)], operands,
        cost_estimate=pl.CostEstimate(flops=20_000_000, bytes_accessed=8_000_000, transcendentals=0),
    )[0]


def local(flow, offsets, intersections, weights):
    span = lax.axis_index("span").astype(jnp.int32).reshape(1)
    one = jax.ShapeDtypeStruct((1,), jnp.int32)
    pm, sm, em, q, *digits = call(
        faces_kernel, "faces", [SMEM, ANY],
        [arr(*FACE), arr(*FACE), arr(2, NB, NR, W), arr(*STATE)] + [one] * 4,
        (offsets, flow),
        [buffer(2, 6, NR, NC), pltpu.SemaphoreType.DMA((2,))],
        [VMEM] * 3 + [ANY] + [SMEM] * 4,
    )
    digits = [d.reshape(()) for d in digits]

    def section(step, carry):
        now, then, q, pm, sm = carry
        at = step.reshape(1), offsets

        def first(d):
            def run(p, s, *rest):
                return both(d)(p, s) + tuple(prep(*rest))
            return run

        p, s, re, le, rad, wb, wf, inv = lax.switch(
            now[0], [first(2 * i) for i in range(8)], pm, sm, *at, span, intersections, flow, q, weights
        )
        radh = lax.ppermute(rad, "span", [(0, 1), (1, 0)])

        def second(d):
            def run(p, s, step, offsets, flow, q, re, le):
                p, s = both(d)(p, s)
                part = bulk(step, flow, q)
                msgs = [arr(NB * 5 + 1, NR, W)] * 2
                return (*call(join_kernel, "join", [SMEM] * 2 + [VMEM] * 4, msgs, (step, offsets, p, s, re, le)), part)
            return run

        mu, md, part = lax.switch(now[1], [second(16 * i) for i in range(8)], p, s, *at, flow, q, re, le)
        up, down = perm(mu, 1), perm(md, -1)
        part = call(
            radial_kernel, "radial", [SMEM] * 2 + [VMEM] * 3, [arr(*STATE)], (at[0], span, part, rad, radh),
            [buffer(10, NP, NC)],
            cost_estimate=pl.CostEstimate(flops=10_000_000, bytes_accessed=4_000_000, transcendentals=0),
        )[0]
        q, pm, sm = call(
            finish_kernel, "finish", [SMEM] * 3 + [ANY] + [VMEM] * 13, [arr(*STATE), arr(*FACE), arr(*FACE)],
            (*at, intersections, q, part, pm, sm, em, mu, md, up, down, re, le, wb, wf, inv),
            [buffer(2 * NB, 5, NR, W), buffer(3 * NB, 40, W)],
            input_output_aliases={3: 0, 5: 1, 6: 2},
        )
        return then, then, q, pm, sm

    return lax.fori_loop(0, 2, section, (tuple(digits[:2]), tuple(digits[2:]), q, pm, sm))[2]


def solution(mesh):
    return jax.shard_map(
        local,
        mesh=mesh,
        in_specs=(P(None, None, None, "span", "sector"), P(), P(), P()),
        out_specs=P(None, None, None, "span", "sector"),
        check_vma=False,
    )
```

```python
import functools

import jax
import jax.numpy as jnp
from jax import lax
from jax.experimental import pallas as pl
from jax.experimental.pallas import tpu as pltpu
from jax.sharding import PartitionSpec as P

VMEM_LIMIT = 16 * 1024 * 1024
NP, NR, NB, W = 8, 8, 4, 128
NC = NB * W


def face(a, b, damping, d):
    s = [x + y for x, y in zip(a, b)]
    inv = 1.0 / s[0]
    u = s[1 + d] * inv
    p = 0.4 * (s[4] - 0.5 * (s[1] * s[1] + s[2] * s[2] + s[3] * s[3]) * inv)
    f = [s[1 + d]] + [s[1 + c] * u + p if c == d else s[1 + c] * u for c in range(3)]
    f.append((s[4] + p) * u)
    return [g - damping * (y - x) for g, x, y in zip(f, a, b)]


def pack_edges(first, flow_ref, q_ref, h, re_ref, le_ref, rad_ref):
    lane = lax.broadcasted_iota(jnp.int32, (NR, W), 1)

    def planes(i, tiles):
        re, le = tiles
        for row in range(2):
            for da in range(2):
                a = 2 * i + da
                for f in range(6):
                    def get(r, c, row=row, a=a, f=f):
                        x = flow_ref[row, f, a, r, c]
                        return x if f == 5 else jnp.where(first, x, q_ref[row, f, a, r, c])
                    at = f * 16 + row * NP + a
                    hit = lane == at
                    re = jnp.where(hit, pltpu.roll(get(slice(None), slice(NC - W, NC)), lax.rem(at + 1, W), 1), re)
                    le = jnp.where(hit, pltpu.roll(get(slice(None), slice(0, W)), at, 1), le)
                    rad_ref[row * 6 + f, pl.ds(a, 1), :] = get(pl.ds(h, 1), slice(None))
        return re, le

    zero = jnp.zeros((NR, W), jnp.float32)
    re_ref[...], le_ref[...] = lax.fori_loop(0, NP // 2, planes, (zero, zero))


def pack_faces(q_ref, pm_ref, sm_ref):
    for b in range(NB):
        for c in range(5):
            pm_ref[b * 5 + c] = q_ref[0, c, NP - 1, :, b * W : (b + 1) * W]
            sm_ref[b * 5 + c] = q_ref[1, c, 0, :, b * W : (b + 1) * W]


def faces_kernel(off_ref, flow_ref, pm_ref, sm_ref, em_ref, q_ref, *rest):
    del q_ref
    step_out, zd_out, ad_out, buf, sem = rest
    cps = [
        pltpu.make_async_copy(flow_ref.at[0, :, NP - 1], buf.at[0], sem.at[0]),
        pltpu.make_async_copy(flow_ref.at[1, :, 0], buf.at[1], sem.at[1]),
    ]
    for cp in cps:
        cp.start()
    even = (off_ref[0] // NB + 1) >> 1
    step_out[0] = 0
    zd_out[0] = even & 7
    ad_out[0] = (even >> 3) & 7
    for cp in cps:
        cp.wait()
    for b in range(NB):
        cells = slice(b * W, (b + 1) * W)
        for c in range(5):
            pm_ref[b * 5 + c] = buf[0, c, :, cells]
            sm_ref[b * 5 + c] = buf[1, c, :, cells]
        em_ref[0, b] = buf[0, 5, :, cells]
        em_ref[1, b] = buf[1, 5, :, cells]


def split(x):
    hi = x.astype(jnp.bfloat16)
    return hi, (x - hi.astype(jnp.float32)).astype(jnp.bfloat16)


def bulk_kernel(step_ref, flow_ref, q_ref, out_ref):
    first_section = step_ref[0] == 0
    half = jnp.where(first_section, 0.0625, 0.125)
    lane = lax.broadcasted_iota(jnp.int32, (NR, W), 1)
    sub = lax.broadcasted_iota(jnp.int32, (NR, NC), 0)

    def no_first(g):
        return jnp.concatenate([jnp.where(lane == 0, 0.0, g[:, :W]), g[:, W:]], axis=1)

    def cells(row, a):
        return [jnp.where(first_section, flow_ref[row, f, a], q_ref[row, f, a]) for f in range(5)]

    for row in range(2):

        def plane(a, carry, row=row):
            x, below = carry
            e = flow_ref[row, 5, a]
            up = jnp.minimum(a + 1, NP - 1)
            following = cells(row, up)
            above = face(x, following, 0.1 + e + flow_ref[row, 5, up], 2)
            if row == 0:
                keep = jnp.where(a == NP - 1, 0.0, 1.0)
                above = [g * keep for g in above]
            total = [g - l for g, l in zip(above, below)]
            lo = [pltpu.roll(v, 1, 0) for v in x]
            g = face(lo, x, 0.1 + e + pltpu.roll(e, 1, 0), 1)
            g = [jnp.where(sub == 0, 0.0, v) for v in g]
            total = [t + (pltpu.roll(v, NR - 1, 0) - v) for t, v in zip(total, g)]
            lo = [pltpu.roll(v, 1, 1) for v in x]
            g = face(lo, x, 0.1 + e + pltpu.roll(e, 1, 1), 0)
            g = [no_first(v) for v in g]
            total = [t + (pltpu.roll(v, NC - 1, 1) - v) for t, v in zip(total, g)]
            for f in range(5):
                out_ref[row, f, a] = flow_ref[row, f, a] - half * total[f]
            return following, above

        x0 = cells(row, 0)
        if row == 0:
            below = face(x0, x0, jnp.zeros((NR, NC), jnp.float32), 2)
        else:
            below = [jnp.zeros((NR, NC), jnp.float32)] * 5
        lax.fori_loop(0, NP, plane, (x0, below))


def edges_kernel(step_ref, span_ref, flow_ref, q_ref, re_ref, le_ref, rad_ref):
    pack_edges(step_ref[0] == 0, flow_ref, q_ref, jnp.where(span_ref[0] == 0, NR - 1, 0), re_ref, le_ref, rad_ref)


def join_kernel(step_ref, off_ref, p_ref, s_ref, re_ref, le_ref, up_ref, down_ref):
    n = 5 * NB
    odd = (off_ref[step_ref[0]] // NB) % 2 == 1
    up_ref[n] = re_ref[...]
    down_ref[n] = le_ref[...]
    for i in range(n):
        up_ref[i] = jnp.where(odd, s_ref[i], p_ref[i])
        down_ref[i] = jnp.where(odd, p_ref[i], s_ref[i])


def middle_kernel(step_ref, off_ref, zd_ref, ad_ref, span_ref, idx_ref, w_hbm, part_ref, rad_ref, radh_ref,
                  step_out, zd_out, ad_out, out_ref, wb_ref, wf_ref, inv_ref, w_ref, acc, sem):
    del zd_ref, ad_ref
    step = step_ref[0]
    offset = off_ref[step]
    get_w = pltpu.make_async_copy(w_hbm.at[step], w_ref, sem)
    get_w.start()
    even = (off_ref[1] // NB + 1) >> 1
    step_out[0] = step + 1
    zd_out[0] = even & 7
    ad_out[0] = (even >> 3) & 7

    half = jnp.where(step == 0, 0.0625, 0.125)
    lower = span_ref[0] == 0
    sgn = jnp.where(lower, 1.0, -1.0)
    at_h = lax.broadcasted_iota(jnp.int32, (NR, NC), 0) == jnp.where(lower, NR - 1, 0)
    for row in range(2):
        own = [rad_ref[row * 6 + f] for f in range(6)]
        other = [radh_ref[row * 6 + f] for f in range(6)]
        g = face(own[:5], other[:5], sgn * (0.1 + own[5] + other[5]), 1)
        for f in range(5):
            fix = (-half * sgn) * g[f]
            for a in range(NP):
                out_ref[row, f, a] = part_ref[row, f, a] + jnp.where(at_h, fix[a : a + 1], 0.0)

    get_w.wait()
    acc[...] = jnp.ones(acc.shape, jnp.float32)
    f0 = offset % NB
    for j in range(NB):
        total = jnp.zeros((8, W), jnp.float32)
        for m in range(2):
            w = w_ref[j, m]
            wt = w.T
            wb_ref[0, j, :, m * W : (m + 1) * W], wb_ref[1, j, :, m * W : (m + 1) * W] = split(w)
            wf_ref[0, j, m * W : (m + 1) * W, :], wf_ref[1, j, m * W : (m + 1) * W, :] = split(wt)
            total = total + jnp.sum(wt, axis=0, keepdims=True)
            d = jnp.sum(w, axis=0, keepdims=True)
            b1 = idx_ref[step, j, m] + 3 - f0
            acc[b1] += d
            acc[b1 + 4] += d
        inv_ref[0, j] = 1.0 / total
    for b in range(NB):
        inv_ref[1, b] = 1.0 / acc[NB + b]


def finish_kernel(step_ref, off_ref, idx_ref, q_hbm, part_ref, pm_ref, sm_ref, em_ref, mu_ref, md_ref, up_ref, down_ref,
                  re_ref, le_ref, wb_ref, wf_ref, inv_ref, out_ref, pm_out, sm_out, win, acc):
    del q_hbm
    step = step_ref[0] - 1
    offset = off_ref[step]
    half = jnp.where(step == 0, 0.0625, 0.125)
    f0 = offset % NB
    odd = (offset // NB) % 2 == 1
    start = NB - 1 - f0
    nface = 5 * NB

    def both_sides(lo, hi):
        lo, hi = ([t if f == 0 else pltpu.roll(t, W - 16 * f, 1) for f in range(6)] for t in (lo, hi))
        return [half * v for v in face(lo[:5], hi[:5], 0.1 + lo[5] + hi[5], 0)]

    left = both_sides(up_ref[nface], le_ref[...])
    right = both_sides(re_ref[...], down_ref[nface])
    lane = lax.broadcasted_iota(jnp.int32, (NR, W), 1)
    for row in range(2):
        for a in range(NP):
            p = row * NP + a
            for f in range(5):
                lo = jnp.where(lane == 0, pltpu.roll(left[f], (W - p) % W, 1), 0.0)
                hi = jnp.where(lane == W - 1, pltpu.roll(right[f], W - 1 - p, 1), 0.0)
                out_ref[row, f, a, :, 0:W] = part_ref[row, f, a, :, 0:W] + lo
                out_ref[row, f, a, :, W : NC - W] = part_ref[row, f, a, :, W : NC - W]
                out_ref[row, f, a, :, NC - W : NC] = part_ref[row, f, a, :, NC - W : NC] - hi

    def dot(x, w_ref, j):
        hi, lo = split(x)
        def one(a, b):
            return jnp.dot(a, b, preferred_element_type=jnp.float32)
        return one(hi, w_ref[0, j]) + (one(hi, w_ref[1, j]) + one(lo, w_ref[0, j]))

    win[NB : 2 * NB] = jnp.where(odd, down_ref[0:nface], mu_ref[0:nface]).reshape(NB, 5, NR, W)
    win[0:NB] = jnp.where(odd, md_ref[0:nface], up_ref[0:nface]).reshape(NB, 5, NR, W)
    acc[...] = jnp.zeros(acc.shape, jnp.float32)
    pad = jnp.zeros((8, W), jnp.float32)
    for j in range(NB):
        lhs = jnp.concatenate(
            [jnp.concatenate([win[start + idx_ref[step, j, m]].reshape(40, W), pad], axis=0) for m in range(2)],
            axis=1,
        )
        num = dot(lhs, wf_ref, j)
        inv = inv_ref[0, j]
        ghost = [num[8 * c : 8 * c + 8] * inv for c in range(5)]
        g = face(ghost, [sm_ref[j * 5 + c] for c in range(5)], 0.1 + 2.0 * em_ref[1, j], 2)
        for c in range(5):
            cells = (1, c, 0, slice(None), slice(j * W, (j + 1) * W))
            out_ref[cells] = out_ref[cells] + half * g[c]
        blk = slice(j * 5, j * 5 + 5)
        s1 = jnp.where(odd, up_ref[blk], md_ref[blk]).reshape(40, W)
        s2 = jnp.where(odd, mu_ref[blk], down_ref[blk]).reshape(40, W)
        r = dot(jnp.concatenate([s1, s2], axis=0), wb_ref, j)
        for m in range(2):
            b1 = idx_ref[step, j, m] + 3 - f0
            acc[b1] += r[0:40, m * W : (m + 1) * W]
            acc[b1 + 4] += r[40:80, m * W : (m + 1) * W]
    for b in range(NB):
        inv = inv_ref[1, b]
        own = [pm_ref[b * 5 + c] for c in range(5)]
        ghost = [(acc[NB + b, 8 * c : 8 * c + 8] + own[c]) * inv for c in range(5)]
        g = face(own, ghost, 0.1 + 2.0 * em_ref[0, b], 2)
        for c in range(5):
            cells = (0, c, NP - 1, slice(None), slice(b * W, (b + 1) * W))
            out_ref[cells] = out_ref[cells] - half * g[c]
    pack_faces(out_ref, pm_out, sm_out)


SMEM = pl.BlockSpec(memory_space=pltpu.SMEM)
VMEM = pl.BlockSpec(memory_space=pltpu.VMEM)
ANY = pl.BlockSpec(memory_space=pl.ANY)
PARAMS = pltpu.CompilerParams(vmem_limit_bytes=VMEM_LIMIT)


def arr(*shape, dtype=jnp.float32):
    return jax.ShapeDtypeStruct(shape, dtype)


def buffer(*shape):
    return pltpu.VMEM(shape, jnp.float32)


FACE = (NB * 5, NR, W)
TILE = (NR, W)
STATE = (2, 5, NP, NR, NC)
HALVES = (2, NB, W, 2 * W)
HALVES_T = (2, NB, 2 * W, W)


def perm(x, d):
    n = lax.axis_size("sector")
    return lax.ppermute(x, "sector", [(i, (i + d) % n) for i in range(n)])


def both(d):
    if d == 0:
        return lambda p, s: (p, s)
    return lambda p, s: (perm(p, d), perm(s, -d))


def call(kernel, name, in_specs, out_shape, operands, scratch=(), out_specs=None, **kw):
    return pl.pallas_call(
        kernel,
        in_specs=in_specs,
        out_specs=out_specs or [VMEM] * len(out_shape),
        out_shape=out_shape,
        scratch_shapes=list(scratch),
        compiler_params=PARAMS,
        name=name,
        **kw,
    )(*operands)


def edges(*operands):
    return call(
        edges_kernel, "edges", [SMEM] * 2 + [VMEM] * 2, [arr(*TILE), arr(*TILE), arr(12, NP, NC)], operands,
        cost_estimate=pl.CostEstimate(flops=10_000_000, bytes_accessed=4_000_000, transcendentals=0),
    )


def bulk(*operands):
    return call(
        bulk_kernel, "bulk", [SMEM] + [VMEM] * 2, [arr(*STATE)], operands,
        cost_estimate=pl.CostEstimate(flops=20_000_000, bytes_accessed=8_000_000, transcendentals=0),
    )[0]


def local(flow, offsets, intersections, weights):
    span = lax.axis_index("span").astype(jnp.int32).reshape(1)
    one = jax.ShapeDtypeStruct((1,), jnp.int32)
    pm, sm, em, q, *state = call(
        faces_kernel, "faces", [SMEM, ANY],
        [arr(*FACE), arr(*FACE), arr(2, NB, NR, W), arr(*STATE)] + [one] * 3,
        (offsets, flow),
        [buffer(2, 6, NR, NC), pltpu.SemaphoreType.DMA((2,))],
        [VMEM] * 3 + [ANY] + [SMEM] * 3,
    )

    def section(_, carry):
        step, zd, ad, q, pm, sm = carry

        def first(d):
            def run(p, s, *rest):
                return both(d)(p, s) + tuple(edges(*rest))
            return run

        p, s, re, le, rad = lax.switch(zd.reshape(()), [first(2 * i) for i in range(8)], pm, sm, step, span, flow, q)
        radh = lax.ppermute(rad, "span", [(0, 1), (1, 0)])

        def second(d):
            def run(p, s, step, offsets, flow, q, re, le):
                p, s = both(d)(p, s)
                part = bulk(step, flow, q)
                msgs = [arr(NB * 5 + 1, NR, W)] * 2
                return (*call(join_kernel, "join", [SMEM] * 2 + [VMEM] * 4, msgs, (step, offsets, p, s, re, le)), part)
            return run

        mu, md, part = lax.switch(
            ad.reshape(()), [second(16 * i) for i in range(8)], p, s, step, offsets, flow, q, re, le
        )
        up, down = perm(mu, 1), perm(md, -1)
        step, zd, ad, part, wb, wf, inv = call(
            middle_kernel, "middle", [SMEM] * 6 + [ANY] + [VMEM] * 3,
            [one] * 3 + [
                arr(*STATE), arr(*HALVES, dtype=jnp.bfloat16), arr(*HALVES_T, dtype=jnp.bfloat16), arr(2, NB, NR, W),
            ],
            (step, offsets, zd, ad, span, intersections, weights, part, rad, radh),
            [buffer(NB, 2, W, W), buffer(3 * NB, NR, W), pltpu.SemaphoreType.DMA],
            [SMEM] * 3 + [VMEM] * 4,
            input_output_aliases={0: 0, 2: 1, 3: 2},
            cost_estimate=pl.CostEstimate(flops=20_000_000, bytes_accessed=8_000_000, transcendentals=0),
        )
        q, pm, sm = call(
            finish_kernel, "finish", [SMEM] * 3 + [ANY] + [VMEM] * 13, [arr(*STATE), arr(*FACE), arr(*FACE)],
            (step, offsets, intersections, q, part, pm, sm, em, mu, md, up, down, re, le, wb, wf, inv),
            [buffer(2 * NB, 5, NR, W), buffer(3 * NB, 40, W)],
            input_output_aliases={3: 0, 5: 1, 6: 2},
        )
        return step, zd, ad, q, pm, sm

    return lax.fori_loop(0, 2, section, (*state, q, pm, sm))[3]


def solution(mesh):
    return jax.shard_map(
        local,
        mesh=mesh,
        in_specs=(P(None, None, None, "span", "sector"), P(), P(), P()),
        out_specs=P(None, None, None, "span", "sector"),
        check_vma=False,
    )
```

```python
import functools

import jax
import jax.numpy as jnp
from jax import lax
from jax.experimental import pallas as pl
from jax.experimental.pallas import tpu as pltpu
from jax.sharding import PartitionSpec as P

VMEM_LIMIT = 16 * 1024 * 1024
NP, NR, NB, W = 8, 8, 4, 128
NC = NB * W


def face(a, b, damping, d):
    s = [x + y for x, y in zip(a, b)]
    inv = 1.0 / s[0]
    u = s[1 + d] * inv
    p = 0.4 * (s[4] - 0.5 * (s[1] * s[1] + s[2] * s[2] + s[3] * s[3]) * inv)
    f = [s[1 + d]] + [s[1 + c] * u + p if c == d else s[1 + c] * u for c in range(3)]
    f.append((s[4] + p) * u)
    return [g - damping * (y - x) for g, x, y in zip(f, a, b)]


def pack_edges(first, lower, flow_ref, q_ref, re_ref, le_ref, rad_ref):
    lane = lax.broadcasted_iota(jnp.int32, (NR, W), 1)

    def planes(i, tiles):
        re, le = tiles
        for row in range(2):
            for da in range(2):
                a = 2 * i + da
                for f in range(6):
                    def get(r, c, row=row, a=a, f=f):
                        x = flow_ref[row, f, a, r, c]
                        return x if f == 5 else jnp.where(first, x, q_ref[row, f, a, r, c])
                    at = f * 16 + row * NP + a
                    hit = lane == at
                    re = jnp.where(hit, pltpu.roll(get(slice(None), slice(NC - W, NC)), lax.rem(at + 1, W), 1), re)
                    le = jnp.where(hit, pltpu.roll(get(slice(None), slice(0, W)), at, 1), le)
                    top, bottom = get(slice(NR - 1, NR), slice(None)), get(slice(0, 1), slice(None))
                    rad_ref[row * 6 + f, pl.ds(a, 1), :] = jnp.where(lower, top, bottom)
        return re, le

    zero = jnp.zeros((NR, W), jnp.float32)
    re_ref[...], le_ref[...] = lax.fori_loop(0, NP // 2, planes, (zero, zero))


def pack_faces(q_ref, pm_ref, sm_ref):
    for b in range(NB):
        for c in range(5):
            pm_ref[b * 5 + c] = q_ref[0, c, NP - 1, :, b * W : (b + 1) * W]
            sm_ref[b * 5 + c] = q_ref[1, c, 0, :, b * W : (b + 1) * W]


def faces_kernel(off_ref, flow_ref, pm_ref, sm_ref, em_ref, q_ref, *rest):
    del q_ref
    digits, (buf, sem) = rest[:4], rest[4:]
    cps = [
        pltpu.make_async_copy(flow_ref.at[0, :, NP - 1], buf.at[0], sem.at[0]),
        pltpu.make_async_copy(flow_ref.at[1, :, 0], buf.at[1], sem.at[1]),
    ]
    for cp in cps:
        cp.start()
    for step in range(2):
        even = (off_ref[step] // NB + 1) >> 1
        digits[2 * step][0] = even & 7
        digits[2 * step + 1][0] = (even >> 3) & 7
    for cp in cps:
        cp.wait()
    for b in range(NB):
        cells = slice(b * W, (b + 1) * W)
        for c in range(5):
            pm_ref[b * 5 + c] = buf[0, c, :, cells]
            sm_ref[b * 5 + c] = buf[1, c, :, cells]
        em_ref[0, b] = buf[0, 5, :, cells]
        em_ref[1, b] = buf[1, 5, :, cells]


def split(x):
    hi = x.astype(jnp.bfloat16)
    return hi, (x - hi.astype(jnp.float32)).astype(jnp.bfloat16)


def bulk_kernel(flag_ref, flow_ref, q_ref, out_ref):
    first_section = jnp.concatenate([flag_ref[0]] * NB, axis=1) > 0.0
    half = jnp.concatenate([flag_ref[2]] * NB, axis=1)
    lane = lax.broadcasted_iota(jnp.int32, (NR, W), 1)
    sub = lax.broadcasted_iota(jnp.int32, (NR, NC), 0)

    def no_first(g):
        return jnp.concatenate([jnp.where(lane == 0, 0.0, g[:, :W]), g[:, W:]], axis=1)

    def cells(row, a):
        return [jnp.where(first_section, flow_ref[row, f, a], q_ref[row, f, a]) for f in range(5)]

    for row in range(2):

        def plane(a, carry, row=row):
            x, below = carry
            e = flow_ref[row, 5, a]
            up = jnp.minimum(a + 1, NP - 1)
            following = cells(row, up)
            above = face(x, following, 0.1 + e + flow_ref[row, 5, up], 2)
            if row == 0:
                keep = jnp.where(a == NP - 1, 0.0, 1.0)
                above = [g * keep for g in above]
            total = [g - l for g, l in zip(above, below)]
            lo = [pltpu.roll(v, 1, 0) for v in x]
            g = face(lo, x, 0.1 + e + pltpu.roll(e, 1, 0), 1)
            g = [jnp.where(sub == 0, 0.0, v) for v in g]
            total = [t + (pltpu.roll(v, NR - 1, 0) - v) for t, v in zip(total, g)]
            lo = [pltpu.roll(v, 1, 1) for v in x]
            g = face(lo, x, 0.1 + e + pltpu.roll(e, 1, 1), 0)
            g = [no_first(v) for v in g]
            total = [t + (pltpu.roll(v, NC - 1, 1) - v) for t, v in zip(total, g)]
            for f in range(5):
                out_ref[row, f, a] = flow_ref[row, f, a] - half * total[f]
            return following, above

        x0 = cells(row, 0)
        if row == 0:
            below = face(x0, x0, jnp.zeros((NR, NC), jnp.float32), 2)
        else:
            below = [jnp.zeros((NR, NC), jnp.float32)] * 5
        lax.fori_loop(0, NP, plane, (x0, below))


def prep_kernel(step_ref, off_ref, span_ref, idx_ref, flow_ref, q_ref, w_hbm, re_ref, le_ref, rad_ref, wb_ref, wf_ref, inv_ref,
                flag_ref, at_ref, w_ref, acc, sem):
    step = step_ref[0]
    offset = off_ref[step]
    get_w = pltpu.make_async_copy(w_hbm.at[step], w_ref, sem)
    get_w.start()
    is_first, is_lower = step == 0, span_ref[0] == 0
    flag_ref[0] = jnp.full(TILE, jnp.where(is_first, 1.0, 0.0))
    flag_ref[1] = jnp.full(TILE, jnp.where((offset // NB) % 2 == 1, 1.0, 0.0))
    flag_ref[2] = jnp.full(TILE, jnp.where(is_first, 0.0625, 0.125))
    flag_ref[3] = jnp.full(TILE, jnp.where(is_lower, 1.0, 0.0))
    for j in range(NB):
        for m in range(2):
            place = idx_ref[step, j, m] + 3 - offset % NB
            at_ref[2 * j + m] = place
    pack_edges(is_first, is_lower, flow_ref, q_ref, re_ref, le_ref, rad_ref)

    get_w.wait()
    acc[...] = jnp.ones(acc.shape, jnp.float32)
    f0 = offset % NB
    for j in range(NB):
        total = jnp.zeros((8, W), jnp.float32)
        for m in range(2):
            w = w_ref[j, m]
            wt = w.T
            wb_ref[0, j, :, m * W : (m + 1) * W], wb_ref[1, j, :, m * W : (m + 1) * W] = split(w)
            wf_ref[0, j, m * W : (m + 1) * W, :], wf_ref[1, j, m * W : (m + 1) * W, :] = split(wt)
            total = total + jnp.sum(wt, axis=0, keepdims=True)
            d = jnp.sum(w, axis=0, keepdims=True)
            b1 = idx_ref[step, j, m] + 3 - f0
            acc[b1] += d
            acc[b1 + 4] += d
        inv_ref[0, j] = 1.0 / total
    for b in range(NB):
        inv_ref[1, b] = 1.0 / acc[NB + b]


def join_kernel(flag_ref, p_ref, s_ref, re_ref, le_ref, up_ref, down_ref):
    n = 5 * NB
    odd = flag_ref[1] > 0.0
    up_ref[n] = re_ref[...]
    down_ref[n] = le_ref[...]
    for i in range(n):
        up_ref[i] = jnp.where(odd, s_ref[i], p_ref[i])
        down_ref[i] = jnp.where(odd, p_ref[i], s_ref[i])


def middle_kernel(flag_ref, part_ref, rad_ref, radh_ref, out_ref):
    half = jnp.concatenate([flag_ref[2]] * NB, axis=1)
    lower = jnp.concatenate([flag_ref[3]] * NB, axis=1)
    sgn = 2.0 * lower - 1.0
    sub = lax.broadcasted_iota(jnp.int32, (NR, NC), 0)
    at_h = sub == jnp.where(lower > 0.0, NR - 1, 0)
    for row in range(2):
        own = [rad_ref[row * 6 + f] for f in range(6)]
        other = [radh_ref[row * 6 + f] for f in range(6)]
        g = face(own[:5], other[:5], sgn * (0.1 + own[5] + other[5]), 1)
        for f in range(5):
            fix = (-half * sgn) * g[f]
            for a in range(NP):
                out_ref[row, f, a] = part_ref[row, f, a] + jnp.where(at_h, fix[a : a + 1], 0.0)


def finish_kernel(at_ref, q_hbm, flag_ref, part_ref, pm_ref, sm_ref, em_ref, mu_ref, md_ref, up_ref, down_ref,
                  re_ref, le_ref, wb_ref, wf_ref, inv_ref, out_ref, pm_out, sm_out, win, acc):
    del q_hbm
    odd = flag_ref[1] > 0.0
    half = flag_ref[2]
    nface = 5 * NB

    def both_sides(lo, hi):
        lo, hi = ([t if f == 0 else pltpu.roll(t, W - 16 * f, 1) for f in range(6)] for t in (lo, hi))
        return [half * v for v in face(lo[:5], hi[:5], 0.1 + lo[5] + hi[5], 0)]

    left = both_sides(up_ref[nface], le_ref[...])
    right = both_sides(re_ref[...], down_ref[nface])
    lane = lax.broadcasted_iota(jnp.int32, (NR, W), 1)
    for row in range(2):
        for a in range(NP):
            p = row * NP + a
            for f in range(5):
                lo = jnp.where(lane == 0, pltpu.roll(left[f], (W - p) % W, 1), 0.0)
                hi = jnp.where(lane == W - 1, pltpu.roll(right[f], W - 1 - p, 1), 0.0)
                out_ref[row, f, a, :, 0:W] = part_ref[row, f, a, :, 0:W] + lo
                out_ref[row, f, a, :, W : NC - W] = part_ref[row, f, a, :, W : NC - W]
                out_ref[row, f, a, :, NC - W : NC] = part_ref[row, f, a, :, NC - W : NC] - hi

    def dot(x, w_ref, j):
        hi, lo = split(x)
        def one(a, b):
            return jnp.dot(a, b, preferred_element_type=jnp.float32)
        return one(hi, w_ref[0, j]) + (one(hi, w_ref[1, j]) + one(lo, w_ref[0, j]))

    win[NB : 2 * NB] = jnp.where(odd, down_ref[0:nface], mu_ref[0:nface]).reshape(NB, 5, NR, W)
    win[0:NB] = jnp.where(odd, md_ref[0:nface], up_ref[0:nface]).reshape(NB, 5, NR, W)
    acc[...] = jnp.zeros(acc.shape, jnp.float32)
    pad = jnp.zeros((8, W), jnp.float32)
    for j in range(NB):
        lhs = jnp.concatenate(
            [jnp.concatenate([win[at_ref[2 * j + m]].reshape(40, W), pad], axis=0) for m in range(2)],
            axis=1,
        )
        num = dot(lhs, wf_ref, j)
        inv = inv_ref[0, j]
        ghost = [num[8 * c : 8 * c + 8] * inv for c in range(5)]
        g = face(ghost, [sm_ref[j * 5 + c] for c in range(5)], 0.1 + 2.0 * em_ref[1, j], 2)
        for c in range(5):
            cells = (1, c, 0, slice(None), slice(j * W, (j + 1) * W))
            out_ref[cells] = out_ref[cells] + half * g[c]
        blk = slice(j * 5, j * 5 + 5)
        s1 = jnp.where(odd, up_ref[blk], md_ref[blk]).reshape(40, W)
        s2 = jnp.where(odd, mu_ref[blk], down_ref[blk]).reshape(40, W)
        r = dot(jnp.concatenate([s1, s2], axis=0), wb_ref, j)
        for m in range(2):
            b1 = at_ref[2 * j + m]
            acc[b1] += r[0:40, m * W : (m + 1) * W]
            acc[b1 + 4] += r[40:80, m * W : (m + 1) * W]
    for b in range(NB):
        inv = inv_ref[1, b]
        own = [pm_ref[b * 5 + c] for c in range(5)]
        ghost = [(acc[NB + b, 8 * c : 8 * c + 8] + own[c]) * inv for c in range(5)]
        g = face(own, ghost, 0.1 + 2.0 * em_ref[0, b], 2)
        for c in range(5):
            cells = (0, c, NP - 1, slice(None), slice(b * W, (b + 1) * W))
            out_ref[cells] = out_ref[cells] - half * g[c]
    pack_faces(out_ref, pm_out, sm_out)


SMEM = pl.BlockSpec(memory_space=pltpu.SMEM)
VMEM = pl.BlockSpec(memory_space=pltpu.VMEM)
ANY = pl.BlockSpec(memory_space=pl.ANY)
PARAMS = pltpu.CompilerParams(vmem_limit_bytes=VMEM_LIMIT)


def arr(*shape, dtype=jnp.float32):
    return jax.ShapeDtypeStruct(shape, dtype)


def buffer(*shape):
    return pltpu.VMEM(shape, jnp.float32)


FACE = (NB * 5, NR, W)
TILE = (NR, W)
STATE = (2, 5, NP, NR, NC)
HALVES = (2, NB, W, 2 * W)
HALVES_T = (2, NB, 2 * W, W)


def perm(x, d):
    n = lax.axis_size("sector")
    return lax.ppermute(x, "sector", [(i, (i + d) % n) for i in range(n)])


def both(d):
    if d == 0:
        return lambda p, s: (p, s)
    return lambda p, s: (perm(p, d), perm(s, -d))


def call(kernel, name, in_specs, out_shape, operands, scratch=(), out_specs=None, **kw):
    return pl.pallas_call(
        kernel,
        in_specs=in_specs,
        out_specs=out_specs or [VMEM] * len(out_shape),
        out_shape=out_shape,
        scratch_shapes=list(scratch),
        compiler_params=PARAMS,
        name=name,
        **kw,
    )(*operands)


def prep(*operands):
    return call(
        prep_kernel, "prep", [SMEM] * 4 + [VMEM] * 2 + [ANY],
        [
            arr(*TILE), arr(*TILE), arr(12, NP, NC),
            arr(*HALVES, dtype=jnp.bfloat16), arr(*HALVES_T, dtype=jnp.bfloat16), arr(2, NB, NR, W),
            arr(4, *TILE), arr(2 * NB, dtype=jnp.int32),
        ],
        operands,
        [buffer(NB, 2, W, W), buffer(3 * NB, NR, W), pltpu.SemaphoreType.DMA],
        [VMEM] * 7 + [SMEM],
        cost_estimate=pl.CostEstimate(flops=10_000_000, bytes_accessed=4_000_000, transcendentals=0),
    )


def bulk(*operands):
    return call(
        bulk_kernel, "bulk", [VMEM] * 3, [arr(*STATE)], operands,
        cost_estimate=pl.CostEstimate(flops=20_000_000, bytes_accessed=8_000_000, transcendentals=0),
    )[0]


def local(flow, offsets, intersections, weights):
    span = lax.axis_index("span").astype(jnp.int32).reshape(1)
    one = jax.ShapeDtypeStruct((1,), jnp.int32)
    pm, sm, em, q, *digits = call(
        faces_kernel, "faces", [SMEM, ANY],
        [arr(*FACE), arr(*FACE), arr(2, NB, NR, W), arr(*STATE)] + [one] * 4,
        (offsets, flow),
        [buffer(2, 6, NR, NC), pltpu.SemaphoreType.DMA((2,))],
        [VMEM] * 3 + [ANY] + [SMEM] * 4,
    )
    digits = [d.reshape(()) for d in digits]

    def section(step, carry):
        now, then, q, pm, sm = carry

        def first(d):
            def run(p, s, *rest):
                return both(d)(p, s) + tuple(prep(*rest))
            return run

        p, s, re, le, rad, wb, wf, inv, flags, places = lax.switch(
            now[0], [first(2 * i) for i in range(8)],
            pm, sm, step.reshape(1), offsets, span, intersections, flow, q, weights,
        )
        radh = lax.ppermute(rad, "span", [(0, 1), (1, 0)])

        def second(d):
            def run(p, s, flags, flow, q, re, le):
                p, s = both(d)(p, s)
                part = bulk(flags, flow, q)
                msgs = [arr(NB * 5 + 1, NR, W)] * 2
                return (*call(join_kernel, "join", [VMEM] * 5, msgs, (flags, p, s, re, le)), part)
            return run

        mu, md, part = lax.switch(now[1], [second(16 * i) for i in range(8)], p, s, flags, flow, q, re, le)
        up, down = perm(mu, 1), perm(md, -1)
        part = call(
            middle_kernel, "middle", [VMEM] * 4, [arr(*STATE)], (flags, part, rad, radh),
            cost_estimate=pl.CostEstimate(flops=20_000_000, bytes_accessed=8_000_000, transcendentals=0),
        )[0]
        q, pm, sm = call(
            finish_kernel, "finish", [SMEM, ANY] + [VMEM] * 14, [arr(*STATE), arr(*FACE), arr(*FACE)],
            (places, q, flags, part, pm, sm, em, mu, md, up, down, re, le, wb, wf, inv),
            [buffer(2 * NB, 5, NR, W), buffer(3 * NB, 40, W)],
            input_output_aliases={1: 0, 4: 1, 5: 2},
        )
        return then, then, q, pm, sm

    return lax.fori_loop(0, 2, section, (tuple(digits[:2]), tuple(digits[2:]), q, pm, sm))[2]


def solution(mesh):
    return jax.shard_map(
        local,
        mesh=mesh,
        in_specs=(P(None, None, None, "span", "sector"), P(), P(), P()),
        out_specs=P(None, None, None, "span", "sector"),
        check_vma=False,
    )
```

```python
import functools

import jax
import jax.numpy as jnp
from jax import lax
from jax.experimental import pallas as pl
from jax.experimental.pallas import tpu as pltpu
from jax.sharding import PartitionSpec as P

VMEM_LIMIT = 16 * 1024 * 1024
NP, NR, NB, W = 8, 8, 4, 128
NC = NB * W


def face(a, b, damping, d):
    s = [x + y for x, y in zip(a, b)]
    inv = 1.0 / s[0]
    u = s[1 + d] * inv
    p = 0.4 * (s[4] - 0.5 * (s[1] * s[1] + s[2] * s[2] + s[3] * s[3]) * inv)
    f = [s[1 + d]] + [s[1 + c] * u + p if c == d else s[1 + c] * u for c in range(3)]
    f.append((s[4] + p) * u)
    return [g - damping * (y - x) for g, x, y in zip(f, a, b)]


def pack_edges(first, lower, flow_ref, q_ref, re_ref, le_ref, rad_ref):
    lane = lax.broadcasted_iota(jnp.int32, (NR, W), 1)

    def planes(i, tiles):
        re, le = tiles
        for row in range(2):
            for da in range(2):
                a = 2 * i + da
                for f in range(6):
                    def get(r, c, row=row, a=a, f=f):
                        x = flow_ref[row, f, a, r, c]
                        return x if f == 5 else jnp.where(first, x, q_ref[row, f, a, r, c])
                    at = f * 16 + row * NP + a
                    hit = lane == at
                    re = jnp.where(hit, pltpu.roll(get(slice(None), slice(NC - W, NC)), lax.rem(at + 1, W), 1), re)
                    le = jnp.where(hit, pltpu.roll(get(slice(None), slice(0, W)), at, 1), le)
                    top, bottom = get(slice(NR - 1, NR), slice(None)), get(slice(0, 1), slice(None))
                    rad_ref[row * 6 + f, pl.ds(a, 1), :] = jnp.where(lower, top, bottom)
        return re, le

    zero = jnp.zeros((NR, W), jnp.float32)
    re_ref[...], le_ref[...] = lax.fori_loop(0, NP // 2, planes, (zero, zero))


def pack_faces(q_ref, pm_ref, sm_ref):
    for b in range(NB):
        for c in range(5):
            pm_ref[b * 5 + c] = q_ref[0, c, NP - 1, :, b * W : (b + 1) * W]
            sm_ref[b * 5 + c] = q_ref[1, c, 0, :, b * W : (b + 1) * W]


def faces_kernel(off_hbm, flow_ref, pm_ref, sm_ref, em_ref, q_ref, *rest):
    del q_ref
    digits, held, (off_ref, buf, sem) = rest[:4], rest[4:8], rest[8:]
    get = pltpu.make_async_copy(off_hbm, off_ref, sem.at[2])
    get.start()
    cps = [
        pltpu.make_async_copy(flow_ref.at[0, :, NP - 1], buf.at[0], sem.at[0]),
        pltpu.make_async_copy(flow_ref.at[1, :, 0], buf.at[1], sem.at[1]),
    ]
    for cp in cps:
        cp.start()
    get.wait()
    for step in range(2):
        even = (off_ref[step] // NB + 1) >> 1
        held[2 * step][0] = even & 7
        held[2 * step + 1][0] = (even >> 3) & 7
    puts = [pltpu.make_async_copy(held[i], digits[i], sem.at[3 + i]) for i in range(4)]
    for cp in puts:
        cp.start()
    for cp in cps:
        cp.wait()
    for b in range(NB):
        cells = slice(b * W, (b + 1) * W)
        for c in range(5):
            pm_ref[b * 5 + c] = buf[0, c, :, cells]
            sm_ref[b * 5 + c] = buf[1, c, :, cells]
        em_ref[0, b] = buf[0, 5, :, cells]
        em_ref[1, b] = buf[1, 5, :, cells]
    for cp in puts:
        cp.wait()


def split(x):
    hi = x.astype(jnp.bfloat16)
    return hi, (x - hi.astype(jnp.float32)).astype(jnp.bfloat16)


def bulk_kernel(flag_ref, flow_ref, q_ref, out_ref):
    first_section = jnp.concatenate([flag_ref[0]] * NB, axis=1) > 0.0
    half = jnp.concatenate([flag_ref[2]] * NB, axis=1)
    lane = lax.broadcasted_iota(jnp.int32, (NR, W), 1)
    sub = lax.broadcasted_iota(jnp.int32, (NR, NC), 0)

    def no_first(g):
        return jnp.concatenate([jnp.where(lane == 0, 0.0, g[:, :W]), g[:, W:]], axis=1)

    def cells(row, a):
        return [jnp.where(first_section, flow_ref[row, f, a], q_ref[row, f, a]) for f in range(5)]

    for row in range(2):

        def plane(a, carry, row=row):
            x, below = carry
            e = flow_ref[row, 5, a]
            up = jnp.minimum(a + 1, NP - 1)
            following = cells(row, up)
            above = face(x, following, 0.1 + e + flow_ref[row, 5, up], 2)
            if row == 0:
                keep = jnp.where(a == NP - 1, 0.0, 1.0)
                above = [g * keep for g in above]
            total = [g - l for g, l in zip(above, below)]
            lo = [pltpu.roll(v, 1, 0) for v in x]
            g = face(lo, x, 0.1 + e + pltpu.roll(e, 1, 0), 1)
            g = [jnp.where(sub == 0, 0.0, v) for v in g]
            total = [t + (pltpu.roll(v, NR - 1, 0) - v) for t, v in zip(total, g)]
            lo = [pltpu.roll(v, 1, 1) for v in x]
            g = face(lo, x, 0.1 + e + pltpu.roll(e, 1, 1), 0)
            g = [no_first(v) for v in g]
            total = [t + (pltpu.roll(v, NC - 1, 1) - v) for t, v in zip(total, g)]
            for f in range(5):
                out_ref[row, f, a] = flow_ref[row, f, a] - half * total[f]
            return following, above

        x0 = cells(row, 0)
        if row == 0:
            below = face(x0, x0, jnp.zeros((NR, NC), jnp.float32), 2)
        else:
            below = [jnp.zeros((NR, NC), jnp.float32)] * 5
        lax.fori_loop(0, NP, plane, (x0, below))


def prep_kernel(step_ref, off_ref, span_ref, idx_ref, flow_ref, q_ref, w_hbm, re_ref, le_ref, rad_ref, wb_ref, wf_ref, inv_ref,
                flag_ref, at_ref, w_ref, acc, sem):
    step = step_ref[0]
    offset = off_ref[step]
    get_w = pltpu.make_async_copy(w_hbm.at[step], w_ref, sem)
    get_w.start()
    is_first, is_lower = step == 0, span_ref[0] == 0
    flag_ref[0] = jnp.full(TILE, jnp.where(is_first, 1.0, 0.0))
    flag_ref[1] = jnp.full(TILE, jnp.where((offset // NB) % 2 == 1, 1.0, 0.0))
    flag_ref[2] = jnp.full(TILE, jnp.where(is_first, 0.0625, 0.125))
    flag_ref[3] = jnp.full(TILE, jnp.where(is_lower, 1.0, 0.0))
    for j in range(NB):
        for m in range(2):
            place = idx_ref[step, j, m] + 3 - offset % NB
            at_ref[2 * j + m] = place
    pack_edges(is_first, is_lower, flow_ref, q_ref, re_ref, le_ref, rad_ref)

    get_w.wait()
    acc[...] = jnp.ones(acc.shape, jnp.float32)
    f0 = offset % NB
    for j in range(NB):
        total = jnp.zeros((8, W), jnp.float32)
        for m in range(2):
            w = w_ref[j, m]
            wt = w.T
            wb_ref[0, j, :, m * W : (m + 1) * W], wb_ref[1, j, :, m * W : (m + 1) * W] = split(w)
            wf_ref[0, j, m * W : (m + 1) * W, :], wf_ref[1, j, m * W : (m + 1) * W, :] = split(wt)
            total = total + jnp.sum(wt, axis=0, keepdims=True)
            d = jnp.sum(w, axis=0, keepdims=True)
            b1 = idx_ref[step, j, m] + 3 - f0
            acc[b1] += d
            acc[b1 + 4] += d
        inv_ref[0, j] = 1.0 / total
    for b in range(NB):
        inv_ref[1, b] = 1.0 / acc[NB + b]


def join_kernel(flag_ref, p_ref, s_ref, re_ref, le_ref, up_ref, down_ref):
    n = 5 * NB
    odd = flag_ref[1] > 0.0
    up_ref[n] = re_ref[...]
    down_ref[n] = le_ref[...]
    for i in range(n):
        up_ref[i] = jnp.where(odd, s_ref[i], p_ref[i])
        down_ref[i] = jnp.where(odd, p_ref[i], s_ref[i])


def middle_kernel(flag_ref, part_ref, rad_ref, radh_ref, out_ref):
    half = jnp.concatenate([flag_ref[2]] * NB, axis=1)
    lower = jnp.concatenate([flag_ref[3]] * NB, axis=1)
    sgn = 2.0 * lower - 1.0
    sub = lax.broadcasted_iota(jnp.int32, (NR, NC), 0)
    at_h = sub == jnp.where(lower > 0.0, NR - 1, 0)
    for row in range(2):
        own = [rad_ref[row * 6 + f] for f in range(6)]
        other = [radh_ref[row * 6 + f] for f in range(6)]
        g = face(own[:5], other[:5], sgn * (0.1 + own[5] + other[5]), 1)
        for f in range(5):
            fix = (-half * sgn) * g[f]
            for a in range(NP):
                out_ref[row, f, a] = part_ref[row, f, a] + jnp.where(at_h, fix[a : a + 1], 0.0)


def finish_kernel(at_ref, q_hbm, flag_ref, part_ref, pm_ref, sm_ref, em_ref, mu_ref, md_ref, up_ref, down_ref,
                  re_ref, le_ref, wb_ref, wf_ref, inv_ref, out_ref, pm_out, sm_out, win, acc):
    del q_hbm
    odd = flag_ref[1] > 0.0
    half = flag_ref[2]
    nface = 5 * NB

    def both_sides(lo, hi):
        lo, hi = ([t if f == 0 else pltpu.roll(t, W - 16 * f, 1) for f in range(6)] for t in (lo, hi))
        return [half * v for v in face(lo[:5], hi[:5], 0.1 + lo[5] + hi[5], 0)]

    left = both_sides(up_ref[nface], le_ref[...])
    right = both_sides(re_ref[...], down_ref[nface])
    lane = lax.broadcasted_iota(jnp.int32, (NR, W), 1)
    for row in range(2):
        for a in range(NP):
            p = row * NP + a
            for f in range(5):
                lo = jnp.where(lane == 0, pltpu.roll(left[f], (W - p) % W, 1), 0.0)
                hi = jnp.where(lane == W - 1, pltpu.roll(right[f], W - 1 - p, 1), 0.0)
                out_ref[row, f, a, :, 0:W] = part_ref[row, f, a, :, 0:W] + lo
                out_ref[row, f, a, :, W : NC - W] = part_ref[row, f, a, :, W : NC - W]
                out_ref[row, f, a, :, NC - W : NC] = part_ref[row, f, a, :, NC - W : NC] - hi

    def dot(x, w_ref, j):
        hi, lo = split(x)
        def one(a, b):
            return jnp.dot(a, b, preferred_element_type=jnp.float32)
        return one(hi, w_ref[0, j]) + (one(hi, w_ref[1, j]) + one(lo, w_ref[0, j]))

    win[NB : 2 * NB] = jnp.where(odd, down_ref[0:nface], mu_ref[0:nface]).reshape(NB, 5, NR, W)
    win[0:NB] = jnp.where(odd, md_ref[0:nface], up_ref[0:nface]).reshape(NB, 5, NR, W)
    acc[...] = jnp.zeros(acc.shape, jnp.float32)
    pad = jnp.zeros((8, W), jnp.float32)
    for j in range(NB):
        lhs = jnp.concatenate(
            [jnp.concatenate([win[at_ref[2 * j + m]].reshape(40, W), pad], axis=0) for m in range(2)],
            axis=1,
        )
        num = dot(lhs, wf_ref, j)
        inv = inv_ref[0, j]
        ghost = [num[8 * c : 8 * c + 8] * inv for c in range(5)]
        g = face(ghost, [sm_ref[j * 5 + c] for c in range(5)], 0.1 + 2.0 * em_ref[1, j], 2)
        for c in range(5):
            cells = (1, c, 0, slice(None), slice(j * W, (j + 1) * W))
            out_ref[cells] = out_ref[cells] + half * g[c]
        blk = slice(j * 5, j * 5 + 5)
        s1 = jnp.where(odd, up_ref[blk], md_ref[blk]).reshape(40, W)
        s2 = jnp.where(odd, mu_ref[blk], down_ref[blk]).reshape(40, W)
        r = dot(jnp.concatenate([s1, s2], axis=0), wb_ref, j)
        for m in range(2):
            b1 = at_ref[2 * j + m]
            acc[b1] += r[0:40, m * W : (m + 1) * W]
            acc[b1 + 4] += r[40:80, m * W : (m + 1) * W]
    for b in range(NB):
        inv = inv_ref[1, b]
        own = [pm_ref[b * 5 + c] for c in range(5)]
        ghost = [(acc[NB + b, 8 * c : 8 * c + 8] + own[c]) * inv for c in range(5)]
        g = face(own, ghost, 0.1 + 2.0 * em_ref[0, b], 2)
        for c in range(5):
            cells = (0, c, NP - 1, slice(None), slice(b * W, (b + 1) * W))
            out_ref[cells] = out_ref[cells] - half * g[c]
    pack_faces(out_ref, pm_out, sm_out)


SMEM = pl.BlockSpec(memory_space=pltpu.SMEM)
VMEM = pl.BlockSpec(memory_space=pltpu.VMEM)
ANY = pl.BlockSpec(memory_space=pl.ANY)
PARAMS = pltpu.CompilerParams(vmem_limit_bytes=VMEM_LIMIT)


def arr(*shape, dtype=jnp.float32):
    return jax.ShapeDtypeStruct(shape, dtype)


def buffer(*shape):
    return pltpu.VMEM(shape, jnp.float32)


FACE = (NB * 5, NR, W)
TILE = (NR, W)
STATE = (2, 5, NP, NR, NC)
HALVES = (2, NB, W, 2 * W)
HALVES_T = (2, NB, 2 * W, W)


def perm(x, d):
    n = lax.axis_size("sector")
    return lax.ppermute(x, "sector", [(i, (i + d) % n) for i in range(n)])


def both(d):
    if d == 0:
        return lambda p, s: (p, s)
    return lambda p, s: (perm(p, d), perm(s, -d))


def call(kernel, name, in_specs, out_shape, operands, scratch=(), out_specs=None, **kw):
    return pl.pallas_call(
        kernel,
        in_specs=in_specs,
        out_specs=out_specs or [VMEM] * len(out_shape),
        out_shape=out_shape,
        scratch_shapes=list(scratch),
        compiler_params=PARAMS,
        name=name,
        **kw,
    )(*operands)


def prep(*operands):
    return call(
        prep_kernel, "prep", [SMEM] * 4 + [VMEM] * 2 + [ANY],
        [
            arr(*TILE), arr(*TILE), arr(12, NP, NC),
            arr(*HALVES, dtype=jnp.bfloat16), arr(*HALVES_T, dtype=jnp.bfloat16), arr(2, NB, NR, W),
            arr(4, *TILE), arr(2 * NB, dtype=jnp.int32),
        ],
        operands,
        [buffer(NB, 2, W, W), buffer(3 * NB, NR, W), pltpu.SemaphoreType.DMA],
        [VMEM] * 7 + [SMEM],
        cost_estimate=pl.CostEstimate(flops=10_000_000, bytes_accessed=4_000_000, transcendentals=0),
    )


def bulk(*operands):
    return call(
        bulk_kernel, "bulk", [VMEM] * 3, [arr(*STATE)], operands,
        cost_estimate=pl.CostEstimate(flops=20_000_000, bytes_accessed=8_000_000, transcendentals=0),
    )[0]


def local(flow, offsets, intersections, weights):
    span = lax.axis_index("span").astype(jnp.int32).reshape(1)
    one = jax.ShapeDtypeStruct((1,), jnp.int32)
    pm, sm, em, q, *digits = call(
        faces_kernel, "faces", [ANY, ANY],
        [arr(*FACE), arr(*FACE), arr(2, NB, NR, W), arr(*STATE)] + [one] * 4,
        (offsets, flow),
        [pltpu.SMEM((1,), jnp.int32)] * 4
        + [pltpu.SMEM((2,), jnp.int32), buffer(2, 6, NR, NC), pltpu.SemaphoreType.DMA((7,))],
        [VMEM] * 3 + [ANY] * 5,
    )
    digits = [d.reshape(()) for d in digits]

    def section(step, carry):
        now, then, q, pm, sm = carry

        def first(d):
            def run(p, s, *rest):
                return both(d)(p, s) + tuple(prep(*rest))
            return run

        p, s, re, le, rad, wb, wf, inv, flags, places = lax.switch(
            now[0], [first(2 * i) for i in range(8)],
            pm, sm, step.reshape(1), offsets, span, intersections, flow, q, weights,
        )
        radh = lax.ppermute(rad, "span", [(0, 1), (1, 0)])

        def second(d):
            def run(p, s, flags, flow, q, re, le):
                p, s = both(d)(p, s)
                part = bulk(flags, flow, q)
                msgs = [arr(NB * 5 + 1, NR, W)] * 2
                return (*call(join_kernel, "join", [VMEM] * 5, msgs, (flags, p, s, re, le)), part)
            return run

        mu, md, part = lax.switch(now[1], [second(16 * i) for i in range(8)], p, s, flags, flow, q, re, le)
        up, down = perm(mu, 1), perm(md, -1)
        part = call(
            middle_kernel, "middle", [VMEM] * 4, [arr(*STATE)], (flags, part, rad, radh),
            cost_estimate=pl.CostEstimate(flops=20_000_000, bytes_accessed=8_000_000, transcendentals=0),
        )[0]
        q, pm, sm = call(
            finish_kernel, "finish", [SMEM, ANY] + [VMEM] * 14, [arr(*STATE), arr(*FACE), arr(*FACE)],
            (places, q, flags, part, pm, sm, em, mu, md, up, down, re, le, wb, wf, inv),
            [buffer(2 * NB, 5, NR, W), buffer(3 * NB, 40, W)],
            input_output_aliases={1: 0, 4: 1, 5: 2},
        )
        return then, then, q, pm, sm

    return lax.fori_loop(0, 2, section, (tuple(digits[:2]), tuple(digits[2:]), q, pm, sm))[2]


def solution(mesh):
    return jax.shard_map(
        local,
        mesh=mesh,
        in_specs=(P(None, None, None, "span", "sector"), P(), P(), P()),
        out_specs=P(None, None, None, "span", "sector"),
        check_vma=False,
    )
```

```python
import functools

import jax
import jax.numpy as jnp
from jax import lax
from jax.experimental import pallas as pl
from jax.experimental.pallas import tpu as pltpu
from jax.sharding import PartitionSpec as P

VMEM_LIMIT = 16 * 1024 * 1024
NP, NR, NB, W = 8, 8, 4, 128
NC = NB * W


def face(a, b, damping, d):
    s = [x + y for x, y in zip(a, b)]
    inv = 1.0 / s[0]
    u = s[1 + d] * inv
    p = 0.4 * (s[4] - 0.5 * (s[1] * s[1] + s[2] * s[2] + s[3] * s[3]) * inv)
    f = [s[1 + d]] + [s[1 + c] * u + p if c == d else s[1 + c] * u for c in range(3)]
    f.append((s[4] + p) * u)
    return [g - damping * (y - x) for g, x, y in zip(f, a, b)]


def pack_edges(first, lower, flow_ref, q_ref, re_ref, le_ref, rad_ref):
    lane = lax.broadcasted_iota(jnp.int32, (NR, W), 1)

    def planes(i, tiles):
        re, le = tiles
        for row in range(2):
            for da in range(2):
                a = 2 * i + da
                for f in range(6):
                    def get(r, c, row=row, a=a, f=f):
                        x = flow_ref[row, f, a, r, c]
                        return x if f == 5 else jnp.where(first, x, q_ref[row, f, a, r, c])
                    at = f * 16 + row * NP + a
                    hit = lane == at
                    re = jnp.where(hit, pltpu.roll(get(slice(None), slice(NC - W, NC)), lax.rem(at + 1, W), 1), re)
                    le = jnp.where(hit, pltpu.roll(get(slice(None), slice(0, W)), at, 1), le)
                    top, bottom = get(slice(NR - 1, NR), slice(None)), get(slice(0, 1), slice(None))
                    rad_ref[row * 6 + f, pl.ds(a, 1), :] = jnp.where(lower, top, bottom)
        return re, le

    zero = jnp.zeros((NR, W), jnp.float32)
    re_ref[...], le_ref[...] = lax.fori_loop(0, NP // 2, planes, (zero, zero))


def pack_faces(q_ref, pm_ref, sm_ref):
    for b in range(NB):
        for c in range(5):
            pm_ref[b * 5 + c] = q_ref[0, c, NP - 1, :, b * W : (b + 1) * W]
            sm_ref[b * 5 + c] = q_ref[1, c, 0, :, b * W : (b + 1) * W]


def faces_kernel(off_hbm, flow_ref, pm_ref, sm_ref, em_ref, q_ref, *rest):
    del q_ref
    digits, held, (off_ref, buf, sem) = rest[:4], rest[4:8], rest[8:]
    get = pltpu.make_async_copy(off_hbm, off_ref, sem.at[2])
    get.start()
    cps = [
        pltpu.make_async_copy(flow_ref.at[0, :, NP - 1], buf.at[0], sem.at[0]),
        pltpu.make_async_copy(flow_ref.at[1, :, 0], buf.at[1], sem.at[1]),
    ]
    for cp in cps:
        cp.start()
    get.wait()
    for step in range(2):
        even = (off_ref[step] // NB + 1) >> 1
        held[2 * step][0] = even & 7
        held[2 * step + 1][0] = (even >> 3) & 7
    puts = [pltpu.make_async_copy(held[i], digits[i], sem.at[3 + i]) for i in range(4)]
    for cp in puts:
        cp.start()
    for cp in cps:
        cp.wait()
    for b in range(NB):
        cells = slice(b * W, (b + 1) * W)
        for c in range(5):
            pm_ref[b * 5 + c] = buf[0, c, :, cells]
            sm_ref[b * 5 + c] = buf[1, c, :, cells]
        em_ref[0, b] = buf[0, 5, :, cells]
        em_ref[1, b] = buf[1, 5, :, cells]
    for cp in puts:
        cp.wait()


def split(x):
    hi = x.astype(jnp.bfloat16)
    return hi, (x - hi.astype(jnp.float32)).astype(jnp.bfloat16)


def bulk_kernel(flag_ref, flow_ref, q_ref, out_ref):
    first_section = jnp.concatenate([flag_ref[0]] * NB, axis=1) > 0.0
    half = jnp.concatenate([flag_ref[2]] * NB, axis=1)
    lane = lax.broadcasted_iota(jnp.int32, (NR, W), 1)
    sub = lax.broadcasted_iota(jnp.int32, (NR, NC), 0)

    def no_first(g):
        return jnp.concatenate([jnp.where(lane == 0, 0.0, g[:, :W]), g[:, W:]], axis=1)

    def cells(row, a):
        return [jnp.where(first_section, flow_ref[row, f, a], q_ref[row, f, a]) for f in range(5)]

    for row in range(2):

        def plane(a, carry, row=row):
            x, below = carry
            e = flow_ref[row, 5, a]
            up = jnp.minimum(a + 1, NP - 1)
            following = cells(row, up)
            above = face(x, following, 0.1 + e + flow_ref[row, 5, up], 2)
            if row == 0:
                keep = jnp.where(a == NP - 1, 0.0, 1.0)
                above = [g * keep for g in above]
            total = [g - l for g, l in zip(above, below)]
            lo = [pltpu.roll(v, 1, 0) for v in x]
            g = face(lo, x, 0.1 + e + pltpu.roll(e, 1, 0), 1)
            g = [jnp.where(sub == 0, 0.0, v) for v in g]
            total = [t + (pltpu.roll(v, NR - 1, 0) - v) for t, v in zip(total, g)]
            lo = [pltpu.roll(v, 1, 1) for v in x]
            g = face(lo, x, 0.1 + e + pltpu.roll(e, 1, 1), 0)
            g = [no_first(v) for v in g]
            total = [t + (pltpu.roll(v, NC - 1, 1) - v) for t, v in zip(total, g)]
            for f in range(5):
                out_ref[row, f, a] = flow_ref[row, f, a] - half * total[f]
            return following, above

        x0 = cells(row, 0)
        if row == 0:
            below = face(x0, x0, jnp.zeros((NR, NC), jnp.float32), 2)
        else:
            below = [jnp.zeros((NR, NC), jnp.float32)] * 5
        lax.fori_loop(0, NP, plane, (x0, below))


def prep_kernel(step_ref, off_ref, span_ref, idx_ref, flow_ref, q_ref, w_hbm, re_ref, le_ref, rad_ref, wb_ref, wf_ref, inv_ref,
                flag_ref, at_ref, w_ref, acc, sem):
    step = step_ref[0]
    offset = off_ref[step]
    get_w = pltpu.make_async_copy(w_hbm.at[step], w_ref, sem)
    get_w.start()
    is_first, is_lower = step == 0, span_ref[0] == 0
    flag_ref[0] = jnp.full(TILE, jnp.where(is_first, 1.0, 0.0))
    flag_ref[1] = jnp.full(TILE, jnp.where((offset // NB) % 2 == 1, 1.0, 0.0))
    flag_ref[2] = jnp.full(TILE, jnp.where(is_first, 0.0625, 0.125))
    flag_ref[3] = jnp.full(TILE, jnp.where(is_lower, 1.0, 0.0))
    for j in range(NB):
        for m in range(2):
            place = idx_ref[step, j, m] + 3 - offset % NB
            at_ref[2 * j + m] = place
    pack_edges(is_first, is_lower, flow_ref, q_ref, re_ref, le_ref, rad_ref)

    get_w.wait()
    acc[...] = jnp.ones(acc.shape, jnp.float32)
    f0 = offset % NB
    for j in range(NB):
        total = jnp.zeros((8, W), jnp.float32)
        for m in range(2):
            w = w_ref[j, m]
            wt = w.T
            wb_ref[0, j, :, m * W : (m + 1) * W], wb_ref[1, j, :, m * W : (m + 1) * W] = split(w)
            wf_ref[0, j, m * W : (m + 1) * W, :], wf_ref[1, j, m * W : (m + 1) * W, :] = split(wt)
            total = total + jnp.sum(wt, axis=0, keepdims=True)
            d = jnp.sum(w, axis=0, keepdims=True)
            b1 = idx_ref[step, j, m] + 3 - f0
            acc[b1] += d
            acc[b1 + 4] += d
        inv_ref[0, j] = 1.0 / total
    for b in range(NB):
        inv_ref[1, b] = 1.0 / acc[NB + b]


def join_kernel(flag_ref, p_ref, s_ref, re_ref, le_ref, up_ref, down_ref):
    n = 5 * NB
    odd = flag_ref[1] > 0.0
    up_ref[n] = re_ref[...]
    down_ref[n] = le_ref[...]
    for i in range(n):
        up_ref[i] = jnp.where(odd, s_ref[i], p_ref[i])
        down_ref[i] = jnp.where(odd, p_ref[i], s_ref[i])


def middle_kernel(flag_ref, part_ref, rad_ref, radh_ref, out_ref):
    half = jnp.concatenate([flag_ref[2]] * NB, axis=1)
    lower = jnp.concatenate([flag_ref[3]] * NB, axis=1)
    sgn = 2.0 * lower - 1.0
    sub = lax.broadcasted_iota(jnp.int32, (NR, NC), 0)
    at_h = sub == jnp.where(lower > 0.0, NR - 1, 0)
    for row in range(2):
        own = [rad_ref[row * 6 + f] for f in range(6)]
        other = [radh_ref[row * 6 + f] for f in range(6)]
        g = face(own[:5], other[:5], sgn * (0.1 + own[5] + other[5]), 1)
        for f in range(5):
            fix = (-half * sgn) * g[f]
            for a in range(NP):
                out_ref[row, f, a] = part_ref[row, f, a] + jnp.where(at_h, fix[a : a + 1], 0.0)


def finish_kernel(at_ref, q_hbm, flag_ref, part_ref, pm_ref, sm_ref, em_ref, mu_ref, md_ref, up_ref, down_ref,
                  re_ref, le_ref, wb_ref, wf_ref, inv_ref, out_ref, pm_out, sm_out, win, acc):
    del q_hbm
    odd = flag_ref[1] > 0.0
    half = flag_ref[2]
    nface = 5 * NB

    def both_sides(lo, hi):
        lo, hi = ([t if f == 0 else pltpu.roll(t, W - 16 * f, 1) for f in range(6)] for t in (lo, hi))
        return [half * v for v in face(lo[:5], hi[:5], 0.1 + lo[5] + hi[5], 0)]

    left = both_sides(up_ref[nface], le_ref[...])
    right = both_sides(re_ref[...], down_ref[nface])
    lane = lax.broadcasted_iota(jnp.int32, (NR, W), 1)
    for row in range(2):
        for a in range(NP):
            p = row * NP + a
            for f in range(5):
                lo = jnp.where(lane == 0, pltpu.roll(left[f], (W - p) % W, 1), 0.0)
                hi = jnp.where(lane == W - 1, pltpu.roll(right[f], W - 1 - p, 1), 0.0)
                out_ref[row, f, a, :, 0:W] = part_ref[row, f, a, :, 0:W] + lo
                out_ref[row, f, a, :, W : NC - W] = part_ref[row, f, a, :, W : NC - W]
                out_ref[row, f, a, :, NC - W : NC] = part_ref[row, f, a, :, NC - W : NC] - hi

    def dot(x, w_ref, j):
        hi, lo = split(x)
        def one(a, b):
            return jnp.dot(a, b, preferred_element_type=jnp.float32)
        return one(hi, w_ref[0, j]) + (one(hi, w_ref[1, j]) + one(lo, w_ref[0, j]))

    win[NB : 2 * NB] = jnp.where(odd, down_ref[0:nface], mu_ref[0:nface]).reshape(NB, 5, NR, W)
    win[0:NB] = jnp.where(odd, md_ref[0:nface], up_ref[0:nface]).reshape(NB, 5, NR, W)
    acc[...] = jnp.zeros(acc.shape, jnp.float32)
    pad = jnp.zeros((8, W), jnp.float32)
    for j in range(NB):
        lhs = jnp.concatenate(
            [jnp.concatenate([win[at_ref[2 * j + m]].reshape(40, W), pad], axis=0) for m in range(2)],
            axis=1,
        )
        num = dot(lhs, wf_ref, j)
        inv = inv_ref[0, j]
        ghost = [num[8 * c : 8 * c + 8] * inv for c in range(5)]
        g = face(ghost, [sm_ref[j * 5 + c] for c in range(5)], 0.1 + 2.0 * em_ref[1, j], 2)
        for c in range(5):
            cells = (1, c, 0, slice(None), slice(j * W, (j + 1) * W))
            out_ref[cells] = out_ref[cells] + half * g[c]
        blk = slice(j * 5, j * 5 + 5)
        s1 = jnp.where(odd, up_ref[blk], md_ref[blk]).reshape(40, W)
        s2 = jnp.where(odd, mu_ref[blk], down_ref[blk]).reshape(40, W)
        r = dot(jnp.concatenate([s1, s2], axis=0), wb_ref, j)
        for m in range(2):
            b1 = at_ref[2 * j + m]
            acc[b1] += r[0:40, m * W : (m + 1) * W]
            acc[b1 + 4] += r[40:80, m * W : (m + 1) * W]
    for b in range(NB):
        inv = inv_ref[1, b]
        own = [pm_ref[b * 5 + c] for c in range(5)]
        ghost = [(acc[NB + b, 8 * c : 8 * c + 8] + own[c]) * inv for c in range(5)]
        g = face(own, ghost, 0.1 + 2.0 * em_ref[0, b], 2)
        for c in range(5):
            cells = (0, c, NP - 1, slice(None), slice(b * W, (b + 1) * W))
            out_ref[cells] = out_ref[cells] - half * g[c]
    pack_faces(out_ref, pm_out, sm_out)


SMEM = pl.BlockSpec(memory_space=pltpu.SMEM)
VMEM = pl.BlockSpec(memory_space=pltpu.VMEM)
ANY = pl.BlockSpec(memory_space=pl.ANY)
PARAMS = pltpu.CompilerParams(vmem_limit_bytes=VMEM_LIMIT)


def arr(*shape, dtype=jnp.float32):
    return jax.ShapeDtypeStruct(shape, dtype)


def buffer(*shape):
    return pltpu.VMEM(shape, jnp.float32)


FACE = (NB * 5, NR, W)
TILE = (NR, W)
STATE = (2, 5, NP, NR, NC)
HALVES = (2, NB, W, 2 * W)
HALVES_T = (2, NB, 2 * W, W)


def perm(x, d):
    n = lax.axis_size("sector")
    return lax.ppermute(x, "sector", [(i, (i + d) % n) for i in range(n)])


def both(d):
    if d == 0:
        return lambda p, s: (p, s)
    return lambda p, s: (perm(p, d), perm(s, -d))


def call(kernel, name, in_specs, out_shape, operands, scratch=(), out_specs=None, **kw):
    return pl.pallas_call(
        kernel,
        in_specs=in_specs,
        out_specs=out_specs or [VMEM] * len(out_shape),
        out_shape=out_shape,
        scratch_shapes=list(scratch),
        compiler_params=PARAMS,
        name=name,
        **kw,
    )(*operands)


def prep(*operands):
    return call(
        prep_kernel, "prep", [SMEM] * 4 + [VMEM] * 2 + [ANY],
        [
            arr(*TILE), arr(*TILE), arr(12, NP, NC),
            arr(*HALVES, dtype=jnp.bfloat16), arr(*HALVES_T, dtype=jnp.bfloat16), arr(2, NB, NR, W),
            arr(4, *TILE), arr(2 * NB, dtype=jnp.int32),
        ],
        operands,
        [buffer(NB, 2, W, W), buffer(3 * NB, NR, W), pltpu.SemaphoreType.DMA],
        [VMEM] * 7 + [SMEM],
        cost_estimate=pl.CostEstimate(flops=10_000_000, bytes_accessed=4_000_000, transcendentals=0),
    )


def bulk(*operands):
    return call(
        bulk_kernel, "bulk", [VMEM] * 3, [arr(*STATE)], operands,
        cost_estimate=pl.CostEstimate(flops=20_000_000, bytes_accessed=8_000_000, transcendentals=0),
    )[0]


def local(flow, offsets, intersections, weights):
    span = lax.axis_index("span").astype(jnp.int32).reshape(1)
    one = jax.ShapeDtypeStruct((1,), jnp.int32)
    pm, sm, em, q, *digits = call(
        faces_kernel, "faces", [ANY, ANY],
        [arr(*FACE), arr(*FACE), arr(2, NB, NR, W), arr(*STATE)] + [one] * 4,
        (offsets, flow),
        [pltpu.SMEM((1,), jnp.int32)] * 4
        + [pltpu.SMEM((2,), jnp.int32), buffer(2, 6, NR, NC), pltpu.SemaphoreType.DMA((7,))],
        [VMEM] * 3 + [ANY] * 5,
    )
    digits = [d.reshape(()) for d in digits]

    def section(step, carry):
        now, then, q, pm, sm = carry

        def first(d):
            def run(p, s, *rest):
                return both(d)(p, s) + tuple(prep(*rest))
            return run

        p, s, re, le, rad, wb, wf, inv, flags, places = lax.switch(
            now[1], [first(16 * i) for i in range(8)],
            pm, sm, step.reshape(1), offsets, span, intersections, flow, q, weights,
        )
        radh = lax.ppermute(rad, "span", [(0, 1), (1, 0)])

        def second(d):
            def run(p, s, flags, flow, q, re, le):
                p, s = both(d)(p, s)
                part = bulk(flags, flow, q)
                msgs = [arr(NB * 5 + 1, NR, W)] * 2
                return (*call(join_kernel, "join", [VMEM] * 5, msgs, (flags, p, s, re, le)), part)
            return run

        mu, md, part = lax.switch(now[0], [second(2 * i) for i in range(8)], p, s, flags, flow, q, re, le)
        up, down = perm(mu, 1), perm(md, -1)
        part = call(
            middle_kernel, "middle", [VMEM] * 4, [arr(*STATE)], (flags, part, rad, radh),
            cost_estimate=pl.CostEstimate(flops=20_000_000, bytes_accessed=8_000_000, transcendentals=0),
        )[0]
        q, pm, sm = call(
            finish_kernel, "finish", [SMEM, ANY] + [VMEM] * 14, [arr(*STATE), arr(*FACE), arr(*FACE)],
            (places, q, flags, part, pm, sm, em, mu, md, up, down, re, le, wb, wf, inv),
            [buffer(2 * NB, 5, NR, W), buffer(3 * NB, 40, W)],
            input_output_aliases={1: 0, 4: 1, 5: 2},
        )
        return then, then, q, pm, sm

    return lax.fori_loop(0, 2, section, (tuple(digits[:2]), tuple(digits[2:]), q, pm, sm))[2]


def solution(mesh):
    return jax.shard_map(
        local,
        mesh=mesh,
        in_specs=(P(None, None, None, "span", "sector"), P(), P(), P()),
        out_specs=P(None, None, None, "span", "sector"),
        check_vma=False,
    )
```
